32 devices in a mesh: fsdp: 8 (over z, x), member: 4 (over y, core).
Axes of the slice: x: 2, y: 2, z: 4, core: 2. Of those that a mesh axis runs over, the one named last changes fastest.
Arguments:
- frames: bfloat16 [4, 1152, 1536], P('member', 'fsdp'), may hold values from -6 to 6
- layer_norm_gain: float32 [1536], replicated, may hold values from 0.25 to 1.75
- input_projection: bfloat16 [1536, 6144], P('fsdp', 'member'), may hold values from -0.15625 to 0.15625
- output_projection: bfloat16 [6144, 1536], P('member', 'fsdp'), may hold values from -0.078125 to 0.078125
- adapter_down_map: bfloat16 [4, 1536, 64], P('member'), may hold values from -0.15625 to 0.15625
- adapter_up_map: bfloat16 [4, 64, 6144], P('member'), may hold values from -0.75 to 0.75
- lengths: int32 [4, 8], P('member', 'fsdp'), may hold values from 90 to 126, as said below
- cotangent: bfloat16 [4, 1152, 1536], P('member', 'fsdp'), may hold values from -0.29882812 to 0.29882812
Outputs:
- down_map_gradient: float32 [4, 1536, 64], P('member')
- up_map_gradient: float32 [4, 64, 6144], P('member')
The draws below stay inside these ranges and needn't reach their ends.
Inputs may be any that keep to these rules, and one draw needn't show every extreme that they name: `lengths`: each member has at least one utterance of exactly 126 frames.
All inputs are finite; a program needn't handle non-finite values.
Results may differ from the reference program's by a relative error of at most 0.0058.
Values may be sent and summed in bfloat16 or wider, within the bound.
No kernel may reach another device: no remote copies, remote signals or barrier semaphores. Data moves between devices by JAX's collectives and lax.ppermute only.
A program may use at most 128 MiB of HBM per device.

```python
import jax
import jax.numpy as jnp
from jax import lax

MODEL_WIDTH = 1536
HIDDEN_UNITS = 6144
ADAPTER_RANK = 64
BUCKET = 144
LMAX = 126
ADJUST_MEMBERS = 4
UTTS = 8
FRAMES = 1152


def draw_lengths(key, part):
    key_len = jax.random.fold_in(key, 11)
    key_pick = jax.random.fold_in(key, 12)
    values = jax.random.randint(key_len, (ADJUST_MEMBERS, UTTS), 5 * BUCKET // 8, LMAX + 1, dtype=jnp.int32)
    chosen = jax.random.randint(key_pick, (ADJUST_MEMBERS,), 0, UTTS, dtype=jnp.int32)
    slots = jnp.arange(UTTS, dtype=jnp.int32)[None, :]
    return jnp.where(slots == chosen[:, None], jnp.int32(LMAX), values)


def shard_levels(key, shape, shards, least, top_value):
    def one(position, shards_of):
        heights = jax.random.uniform(jax.random.fold_in(jax.random.fold_in(key, 6), position), (shards_of,), jnp.float32, least / len(shards), top_value / len(shards))
        return jnp.repeat(jnp.exp(heights), shape[position] // shards_of).reshape((-1,) + (1,) * (len(shape) - position - 1))

    loudness = one(*shards[0])
    for cut in shards[1:]:
        loudness = loudness * one(*cut)
    return loudness


def gaussian(rng, shape, scale, limit, cuts=(), kind=jnp.bfloat16):
    values = jax.random.normal(rng, shape, jnp.float32) * scale
    if len(cuts) > 0:
        values = shard_levels(rng, shape, cuts, -0.22, 0.18) * values
    return jnp.clip(values, min=-limit, max=limit).astype(kind)


def setup_inputs(seed: int = 0) -> dict:
    seeds = jax.random.split(jax.random.key(seed), 9)
    return {
        "frames": gaussian(seeds[0], (ADJUST_MEMBERS, FRAMES, MODEL_WIDTH), 1.0, 6.0, ((0, 4), (1, 8))),
        "layer_norm_gain": jnp.clip(1.0 + 0.15 * jax.random.normal(seeds[1], (MODEL_WIDTH,), jnp.float32), 0.25, 1.75),
        "input_projection": gaussian(seeds[2], (MODEL_WIDTH, HIDDEN_UNITS), MODEL_WIDTH ** -0.5, 0.15625, ((0, 8), (1, 4))),
        "output_projection": gaussian(seeds[3], (HIDDEN_UNITS, MODEL_WIDTH), HIDDEN_UNITS ** -0.5, 0.078125, ((0, 4), (1, 8))),
        "adapter_down_map": gaussian(seeds[4], (ADJUST_MEMBERS, MODEL_WIDTH, ADAPTER_RANK), MODEL_WIDTH ** -0.5, 0.15625, ((0, 4),)),
        "adapter_up_map": gaussian(seeds[5], (ADJUST_MEMBERS, ADAPTER_RANK, HIDDEN_UNITS), ADAPTER_RANK ** -0.5, 0.75, ((0, 4),)),
        "lengths": draw_lengths(jax.random.fold_in(seeds[8], 71), 0),
        "cotangent": gaussian(seeds[7], (ADJUST_MEMBERS, FRAMES, MODEL_WIDTH), 0.05, 0.29882812, ((0, 4), (1, 8))),
    }


def reference(frames, layer_norm_gain, input_projection, output_projection, adapter_down_map, adapter_up_map, lengths, cotangent):
    positions = jnp.arange(BUCKET, dtype=jnp.int32)

    def member_gradient_list(packed):
        block, down, up, sizes, cot = packed
        values = block.astype(jnp.float32)
        mean = lax.optimization_barrier(jnp.mean(values, axis=1, keepdims=True))
        var = lax.optimization_barrier(jnp.mean((values - mean) ** 2, axis=1, keepdims=True))
        normed_input = (layer_norm_gain * (values - mean) / jnp.sqrt(var + 1e-05)).astype(jnp.bfloat16)
        low_rank_state = jnp.dot(normed_input, down, preferred_element_type=jnp.float32).astype(jnp.bfloat16)
        pre = jnp.dot(normed_input, input_projection, preferred_element_type=jnp.float32) + jnp.dot(low_rank_state, up, preferred_element_type=jnp.float32)
        mask = (positions[None, :] < sizes[:, None]).reshape(-1)
        masked = cot * mask.astype(cot.dtype)[:, None]
        dhid = 0.5 * jnp.dot(masked, output_projection.T, preferred_element_type=jnp.float32)
        sig = jax.nn.sigmoid(pre)
        dpre = (dhid * sig * (1.0 + pre * (1.0 - sig))).astype(jnp.bfloat16)
        up_map_gradient = jnp.dot(low_rank_state.T, dpre, preferred_element_type=jnp.float32)
        back = jnp.dot(dpre, up.T, preferred_element_type=jnp.float32).astype(jnp.bfloat16)
        down_map_gradient = jnp.dot(normed_input.T, back, preferred_element_type=jnp.float32)
        return (down_map_gradient, up_map_gradient)
    down_map_gradient, up_map_gradient = lax.map(member_gradient_list, (frames, adapter_down_map, adapter_up_map, lengths, cotangent))
    return (down_map_gradient, up_map_gradient)
```

```python
import jax
import jax.numpy as jnp
from jax import lax
from jax.sharding import PartitionSpec as P

BUCKET = 144
LMAX = 126
BF = jnp.bfloat16
F32 = jnp.float32


def normalize(frames, gain):
    values = frames.astype(F32)
    mean = jnp.mean(values, axis=1, keepdims=True)
    var = jnp.mean((values - mean) ** 2, axis=1, keepdims=True)
    return (gain * (values - mean) / jnp.sqrt(var + 1e-05)).astype(BF)


def swish_gradient(pre, dhid):
    sigma = jax.nn.sigmoid(pre)
    return (dhid * sigma * (1.0 + pre * (1.0 - sigma))).astype(BF)


def dot(a, b, dims=((1,), (0,))):
    return lax.dot_general(a, b, (dims, ((), ())), preferred_element_type=F32)


def flip(axis, size, bits):
    return lambda value: lax.ppermute(value, axis, [(i, i ^ bits) for i in range(size)])


def paired_halves(frames, gain, first, second, down_map, up_map, lengths, cotangent):
    f, m = lax.axis_index("fsdp"), lax.axis_index("member")
    low_bit, x = (f >> 1) & 1, f & 1
    y, core = m >> 1, m & 1
    over_x, over_low = flip("fsdp", 8, 1), flip("fsdp", 8, 2)
    over_half, over_both = flip("fsdp", 8, 4), flip("fsdp", 8, 6)
    over_xlow = flip("fsdp", 8, 3)
    over_y, over_core = flip("member", 4, 2), flip("member", 4, 1)

    width = frames.shape[2]
    rank = down_map.shape[2]
    rows = -(-LMAX // 16) * 16
    depth, block = first.shape
    part = block // 4

    normed = normalize(frames[0, :rows], gain)
    low = dot(normed, down_map[0]).astype(BF)
    keep = jnp.arange(rows, dtype=jnp.int32)[:, None] < lengths[0, 0]
    masked = cotangent[0, :rows] * keep.astype(BF)
    own = jnp.concatenate([normed, masked, low, jnp.zeros_like(low)], axis=1)

    both = jnp.concatenate([first, second.T], axis=0)

    def piece(dx, dl):
        return lax.dynamic_slice(both, (0, ((x ^ dx) * 2 + (low_bit ^ dl)) * part), (2 * depth, part))

    w00, w01 = piece(0, 0), piece(0, 1)
    wx = over_x(jnp.stack([piece(1, 0), piece(1, 1)]))
    near = [w00, over_low(w01), over_half(w00), over_both(w01)]
    far = [wx[0], over_low(wx[1]), over_half(wx[0]), over_both(wx[1])]
    pieces = jnp.stack([near[0], far[0], near[1], far[1], near[2], far[2], near[3], far[3]])
    other = over_core(pieces)
    order = f ^ jnp.arange(8)
    mine_first = jnp.concatenate([pieces, other], axis=2)
    weights = jnp.take(mine_first, order, axis=0)
    w_in = weights[:, :depth].reshape(8 * depth, 2 * part)
    w_out = weights[:, depth:].reshape(8 * depth, 2 * part)

    def columns(ym):
        return jnp.concatenate(
            [
                lax.dynamic_slice(
                    up_map[0], (0, (ym * 2 + (core ^ dc)) * block + (x * 2 + low_bit) * part), (rank, part)
                )
                for dc in range(2)
            ],
            axis=1,
        )

    maps = [columns(y), over_y(columns(1 - y))]

    fz, fx, fy = over_low(own), over_x(own), over_y(own)
    fzx, fzy = over_x(fz), over_y(fz)
    fxy = jnp.concatenate([over_x(fy[:, :width]), over_y(fx[:, width:])], axis=1)
    fzxy = over_y(fzx)
    slots = (low_bit * 2 + x) ^ jnp.arange(4)
    members = [
        jnp.take(jnp.stack([own, fx, fz, fzx]), slots, axis=0).reshape(4 * rows, -1),
        jnp.take(jnp.stack([fy, fxy, fzy, fzxy]), slots, axis=0).reshape(4 * rows, -1),
    ]

    ups, backs = [], []
    for packed, up in zip(members, maps):
        n, c, a = packed[:, :width], packed[:, width : 2 * width], packed[:, 2 * width : 2 * width + rank]
        pre = dot(n, w_in) + dot(a, up)
        dhid = 0.5 * dot(c, w_out)
        dpre = swish_gradient(pre, dhid)
        ups.append(dot(a, dpre, ((0,), (0,))))
        backs.append(dot(up, dpre, ((1,), (1,))))

    got = over_y(jnp.concatenate([ups[1], backs[1]], axis=1).astype(BF))
    hidden = 2 * part
    back = (backs[0] + got[:, hidden:].astype(F32)).astype(BF)
    bx, bz, bzx = over_x(back), over_low(back), over_xlow(back)
    up_pair = jnp.stack([ups[0].astype(BF), got[:, :hidden]])
    up_half = over_half(up_pair)
    up_sum = (up_pair.astype(F32) + up_half.astype(F32)).astype(BF)
    back_sum = (
        (back.astype(F32) + bx.astype(F32)) + (bz.astype(F32) + bzx.astype(F32))
    ).astype(BF)
    down = dot(members[0][:, :width], back_sum, ((0,), (1,))).astype(BF)
    down_other = over_half(down)
    ux, uz, uzx = over_x(up_sum), over_low(up_sum), over_xlow(up_sum)
    down_sum = down.astype(F32) + down_other.astype(F32)
    parts = jnp.take(jnp.stack([up_sum, uz, ux, uzx]), (x * 2 + low_bit) ^ jnp.arange(4), axis=0)
    parts = jnp.take(parts, y ^ jnp.arange(2), axis=1)
    parts = parts.reshape(4, 2, rank, 2, part)
    parts = jnp.take(parts, core ^ jnp.arange(2), axis=3)
    up_sum = parts.transpose(2, 1, 3, 0, 4).reshape(rank, -1).astype(F32)
    return (down_sum[None], up_sum[None])


def gathered(frames, gain, first, second, down_map, up_map, lengths, cotangent):
    members = lax.axis_size("member")
    normed = normalize(frames[0], gain)
    low = dot(normed, down_map[0]).astype(BF)
    positions = jnp.arange(BUCKET, dtype=jnp.int32)
    mask = (positions[None, :] < lengths[0][:, None]).reshape(-1)
    masked = cotangent[0] * mask.astype(BF)[:, None]
    rows = normed.shape[0]
    up_slices = lax.all_to_all(up_map, "member", split_axis=2, concat_axis=0, tiled=True)
    all_normed = lax.all_gather(normed, "member", axis=0, tiled=True)
    all_low = lax.all_gather(low, "member", axis=0, tiled=True).reshape(members, rows, -1)
    all_masked = lax.all_gather(masked, "member", axis=0, tiled=True)
    term = jnp.einsum("dgs,dsb->dgb", all_low, up_slices, preferred_element_type=F32)
    pre = term.reshape(members * rows, -1) + dot(
        all_normed, lax.all_gather(first, "fsdp", axis=0, tiled=True)
    )
    dhid = 0.5 * dot(all_masked, lax.all_gather(second, "fsdp", axis=1, tiled=True), ((1,), (1,)))
    dpre = swish_gradient(pre, dhid).reshape(members, rows, -1)
    up_partial = jnp.einsum("jnz,jnv->jzv", all_low, dpre, preferred_element_type=F32)
    back_partial = jnp.einsum("yha,ywa->yhw", dpre, up_slices, preferred_element_type=F32)
    back = lax.psum_scatter(back_partial, "member", scatter_dimension=0, tiled=True)[0].astype(BF)
    up = lax.all_to_all(lax.psum(up_partial, "fsdp"), "member", split_axis=0, concat_axis=2, tiled=True)
    down = lax.psum(dot(normed, back, ((0,), (0,))), "fsdp")
    return (down[None], up)


def solution(mesh):
    in_specs = (
        P("member", "fsdp", None),
        P(),
        P("fsdp", "member"),
        P("member", "fsdp"),
        P("member", None, None),
        P("member", None, None),
        P("member", "fsdp"),
        P("member", "fsdp", None),
    )
    out_specs = (P("member", None, None), P("member", None, None))
    paired = mesh.shape["fsdp"] == 8 and mesh.shape["member"] == 4
    return jax.shard_map(
        paired_halves if paired else gathered,
        mesh=mesh,
        in_specs=in_specs,
        out_specs=out_specs,
        check_vma=False,
    )
```

```python
import jax
import jax.numpy as jnp
from jax import lax
from jax.experimental import pallas as pl
from jax.experimental.pallas import tpu as pltpu
from jax.sharding import PartitionSpec as P

BUCKET = 144
LMAX = 126
BF = jnp.bfloat16
F32 = jnp.float32


def normalize(frames, gain):
    values = frames.astype(F32)
    mean = jnp.mean(values, axis=1, keepdims=True)
    var = jnp.mean((values - mean) ** 2, axis=1, keepdims=True)
    return (gain * (values - mean) / jnp.sqrt(var + 1e-05)).astype(BF)


def swish_gradient(pre, dhid):
    sigma = jax.nn.sigmoid(pre)
    return (dhid * sigma * (1.0 + pre * (1.0 - sigma))).astype(BF)


def dot(a, b, dims=((1,), (0,))):
    return lax.dot_general(a, b, (dims, ((), ())), preferred_element_type=F32)


def flip(axis, size, bits):
    return lambda value: lax.ppermute(value, axis, [(i, i ^ bits) for i in range(size)])


def whole(shape):
    return pl.BlockSpec(shape, lambda: (0,) * len(shape))


def place():
    f, m = lax.axis_index("fsdp"), lax.axis_index("member")
    return f, (f >> 1) & 1, f & 1, m >> 1, m & 1


def lanes(start, size):
    return pl.ds(pl.multiple_of(start, 128), size)


def call(body, ins, outs, args, scratch=(), flops=0):
    size = sum(a.size * a.dtype.itemsize for a in args)
    return pl.pallas_call(
        body,
        in_specs=ins,
        out_specs=[whole(o.shape) for o in outs],
        out_shape=outs,
        scratch_shapes=list(scratch),
        compiler_params=pltpu.CompilerParams(vmem_limit_bytes=40 * 1024 * 1024),
        cost_estimate=pl.CostEstimate(flops=flops, bytes_accessed=size, transcendentals=0),
    )(*args)


def cut_weights(first, second):
    depth, block = first.shape
    part = block // 4
    piece = jax.ShapeDtypeStruct((2 * depth, part), BF)
    pair = jax.ShapeDtypeStruct((2, 2 * depth, part), BF)

    def body(first_ref, second_ref, away_ref, same_ref, flip_ref):
        _, low_bit, x, _, _ = place()
        for dx in (1, 0):
            for dl in (0, 1):
                start = ((x ^ dx) * 2 + (low_bit ^ dl)) * part
                out = away_ref.at[dl] if dx else (same_ref, flip_ref)[dl]
                out[:depth] = first_ref[:, lanes(start, part)]
                out[depth:] = second_ref[lanes(start, part), :].T

    return call(body, [whole(first.shape), whole(second.shape)], [pair, piece, piece], (first, second))


def pack_frames(frames, gain, down_map, up_map, lengths, cotangent, rows, part):
    width, rank = frames.shape[2], down_map.shape[2]
    fold = rank // 16
    lined = 2 * width + 2 * rank

    def body(frames_ref, gain_ref, down_ref, up_ref, lengths_ref, cot_ref, own_ref, cross_ref):
        _, low_bit, x, y, core = place()
        normed = normalize(frames_ref[0, :rows], gain_ref[...])
        keep = lax.broadcasted_iota(jnp.int32, (rows, width), 0) < lengths_ref[0, 0]
        masked = jnp.where(keep, cot_ref[0, :rows].astype(F32), 0.0).astype(BF)
        low = dot(normed, down_ref[0])
        low = jnp.concatenate([low, jnp.zeros_like(low)], axis=1).astype(BF)
        for ref in (own_ref, cross_ref):
            ref[:rows, :width] = normed
            ref[:rows, width : 2 * width] = masked
            ref[:rows, 2 * width :] = low
        for dc in range(2):
            start = ((1 - y) * 2 + (core ^ dc)) * (4 * part) + (x * 2 + low_bit) * part
            columns = up_ref[0, :, lanes(start, part)]
            for i in range(fold):
                at = (2 * i + dc) * part
                cross_ref[rows:, at : at + part] = columns[16 * i : 16 * (i + 1)]
        cross_ref[rows:, 2 * fold * part :] = jnp.zeros((16, lined - 2 * fold * part), BF)

    args = (frames, gain[None], down_map, up_map, lengths, cotangent)
    ins = [whole(a.shape) for a in args]
    ins[4] = pl.BlockSpec(memory_space=pltpu.SMEM)
    outs = [jax.ShapeDtypeStruct((n, lined), BF) for n in (rows, rows + 16)]
    return call(body, ins, outs, args, flops=2 * rows * width * rank)


def work(pieces, swapped, frames, up, width, rank, own):
    depth, part = pieces[0].shape[0] // 2, pieces[0].shape[1]
    rows = frames[1].shape[0]
    lined = frames[1].shape[1]
    codes = (0, 1, 2, 4, 6, 3, 5, 7)
    n_pieces, n_swapped = len(pieces), len(swapped)
    hidden = 2 * part
    count = 4 * rows
    kind = F32 if own else BF

    def body(*refs):
        piece_refs, refs = refs[:n_pieces], refs[n_pieces:]
        swap_refs, refs = refs[:n_swapped], refs[n_swapped:]
        frame_refs, refs = refs[:4], refs[4:]
        (up_ref, out_ref, w_in, w_out, packed, map_ref, sems, frame_sems), = (refs,)
        f, low_bit, x, y, core = place()
        slot = low_bit * 2 + x
        copies = []
        loads = []
        for i, ref in enumerate(frame_refs):
            at = pl.multiple_of((slot ^ i) * rows, 16)
            loads.append(
                pltpu.make_async_copy(ref.at[pl.ds(0, rows)], packed.at[pl.ds(at, rows)], frame_sems.at[i])
            )
        flat = [r.at[j] if len(r.shape) == 3 else r for r in swap_refs for j in range(r.shape[0] if len(r.shape) == 3 else 1)]
        for side, group in enumerate((piece_refs, flat)):
            for i, ref in enumerate(group):
                at = pl.multiple_of((f ^ codes[i]) * depth, 16)
                for k, w in enumerate((w_in, w_out)):
                    copies.append(
                        pltpu.make_async_copy(
                            ref.at[pl.ds(k * depth, depth)],
                            w.at[pl.ds(at, depth), pl.ds(side * part, part)],
                            sems.at[len(copies)],
                        )
                    )
        for copy in loads + copies:
            copy.start()
        if own:
            for dc in range(2):
                start = (y * 2 + (core ^ dc)) * (4 * part) + (x * 2 + low_bit) * part
                map_ref[:, dc * part : (dc + 1) * part] = up_ref[0, :, lanes(start, part)]
        else:
            for i in range(rank // 16):
                map_ref[16 * i : 16 * (i + 1), :] = up_ref[rows:, i * hidden : (i + 1) * hidden]
        for copy in loads + copies:
            copy.wait()
        step = 256 if hidden % 256 == 0 else part
        back = jnp.zeros((rank, count), F32)
        low = packed[:, 2 * width :][:, :rank]
        for at in range(0, hidden, step):
            now = slice(at, at + step)
            pre = dot(packed[:, :width], w_in[:, now]) + dot(low, map_ref[:, now])
            dhid = 0.5 * dot(packed[:, width : 2 * width], w_out[:, now])
            dpre = swish_gradient(pre, dhid)
            out_ref[:, now] = dot(low, dpre, ((0,), (0,))).astype(kind)
            back = back + dot(map_ref[:, now], dpre, ((1,), (1,)))
        out_ref[:, hidden:] = back.astype(kind)

    args = (*pieces, *swapped, *frames, up)
    anywhere = pl.BlockSpec(memory_space=pl.ANY)
    ins = [anywhere] * (len(args) - 1) + [whole(up.shape)]
    scratch = [
        pltpu.VMEM((8 * depth, hidden), BF),
        pltpu.VMEM((8 * depth, hidden), BF),
        pltpu.VMEM((count, lined), BF),
        pltpu.VMEM((rank, hidden), BF),
        pltpu.SemaphoreType.DMA((32,)),
        pltpu.SemaphoreType.DMA((4,)),
    ]
    outs = [jax.ShapeDtypeStruct((rank, hidden + count), kind)]
    return call(body, ins, outs, args, scratch, flops=4 * count * 8 * depth * hidden)[0]


def spread(parts, down, down_other, block):
    _, rank, hidden = parts[0].shape
    part = hidden // 2

    def body(*refs):
        part_refs, (down_ref, other_ref, up_out, down_out) = refs[:4], refs[4:]
        _, low_bit, x, y, core = place()
        slot = x * 2 + low_bit
        for i, ref in enumerate(part_refs):
            for dy in range(2):
                for dc in range(2):
                    start = ((y ^ dy) * 2 + (core ^ dc)) * block + (slot ^ i) * part
                    up_out[0, :, lanes(start, part)] = ref[dy, :, dc * part : (dc + 1) * part].astype(F32)
        down_out[0] = down_ref[...].astype(F32) + other_ref[...].astype(F32)

    args = (*parts, down, down_other)
    outs = [
        jax.ShapeDtypeStruct((1, rank, 4 * block), F32),
        jax.ShapeDtypeStruct((1, *down.shape), F32),
    ]
    return call(body, [whole(a.shape) for a in args], outs, args)


def after(value, *done):
    return lax.optimization_barrier((value, *done))[0]


def paired_halves(frames, gain, first, second, down_map, up_map, lengths, cotangent):
    over_x, over_low = flip("fsdp", 8, 1), flip("fsdp", 8, 2)
    over_half, over_both = flip("fsdp", 8, 4), flip("fsdp", 8, 6)
    over_xlow = flip("fsdp", 8, 3)
    over_y, over_core = flip("member", 4, 2), flip("member", 4, 1)

    width, rank = frames.shape[2], down_map.shape[2]
    rows = -(-LMAX // 16) * 16
    block = first.shape[1]
    part = block // 4
    hidden = 2 * part

    away, w00, w01 = cut_weights(first, second)
    wx = over_x(away)
    z2n = over_half(w00)
    own, cross = pack_frames(frames, gain, down_map, up_map, lengths, cotangent, rows, part)
    fy = over_y(cross)
    fz = over_low(own)
    fx = over_x(after(own, wx))
    z3n = over_both(after(w01, z2n))
    z1n = over_low(after(w01, fz))
    wx0, wx1 = wx[0], wx[1]
    z1f = over_low(after(wx1, z1n))
    fzy = over_y(after(fz, fy))
    z2f = over_half(after(wx0, z3n))
    group1 = over_core(jnp.stack([w00, wx0, z1n, z2n]))
    fzx = over_x(after(fz, fx))
    fxy = over_y(after(fx, fzy))
    z3f = over_both(after(wx1, z2f))
    group2 = over_core(jnp.stack([z3n, z1f, z2f]))
    cut = rows * 5 // 8 // 16 * 16
    fzxy_a = over_x(after(fzy[:cut], fzx))
    fzxy_b = over_y(after(fzx[cut:], fxy))
    group3 = over_core(after(z3f, group2))
    pieces = [w00, wx0, z1n, z2n, z3n, z1f, z2f, z3f]
    swapped = [group1, group2, group3]

    mine = work(pieces, swapped, [own, fx, fz, fzx], up_map, width, rank, True)
    fzxy = jnp.concatenate([fzxy_a, fzxy_b], axis=0)
    theirs = work(pieces, swapped, [fy, fxy, fzy, fzxy], fy, width, rank, False)

    got = over_y(theirs)
    back = (mine[:, hidden:] + got[:, hidden:].astype(F32)).astype(BF)
    bx, bz, bzx = over_x(back), over_low(back), over_xlow(back)
    up_pair = jnp.stack([mine[:, :hidden].astype(BF), got[:, :hidden]])
    up_half = over_half(up_pair)
    up_sum = (up_pair.astype(F32) + up_half.astype(F32)).astype(BF)
    back_sum = (
        (back.astype(F32) + bx.astype(F32)) + (bz.astype(F32) + bzx.astype(F32))
    ).astype(BF)
    slots = (lax.axis_index("fsdp") & 3) ^ jnp.arange(4)
    normed = jnp.take(jnp.stack([v[:, :width] for v in (own, fx, fz, fzx)]), slots, axis=0)
    down = dot(normed.reshape(4 * rows, width), back_sum, ((0,), (1,))).astype(BF)
    down_other = over_half(down)
    ux, uz, uzx = over_x(up_sum), over_low(up_sum), over_xlow(up_sum)
    up_gradient, down_gradient = spread([up_sum, uz, ux, uzx], down, down_other, block)
    return (down_gradient, up_gradient)


def gathered(frames, gain, first, second, down_map, up_map, lengths, cotangent):
    members = lax.axis_size("member")
    normed = normalize(frames[0], gain)
    low = dot(normed, down_map[0]).astype(BF)
    positions = jnp.arange(BUCKET, dtype=jnp.int32)
    mask = (positions[None, :] < lengths[0][:, None]).reshape(-1)
    masked = cotangent[0] * mask.astype(BF)[:, None]
    rows = normed.shape[0]
    up_slices = lax.all_to_all(up_map, "member", split_axis=2, concat_axis=0, tiled=True)
    all_normed = lax.all_gather(normed, "member", axis=0, tiled=True)
    all_low = lax.all_gather(low, "member", axis=0, tiled=True).reshape(members, rows, -1)
    all_masked = lax.all_gather(masked, "member", axis=0, tiled=True)
    term = jnp.einsum("dgs,dsb->dgb", all_low, up_slices, preferred_element_type=F32)
    pre = term.reshape(members * rows, -1) + dot(
        all_normed, lax.all_gather(first, "fsdp", axis=0, tiled=True)
    )
    dhid = 0.5 * dot(all_masked, lax.all_gather(second, "fsdp", axis=1, tiled=True), ((1,), (1,)))
    dpre = swish_gradient(pre, dhid).reshape(members, rows, -1)
    up_partial = jnp.einsum("jnz,jnv->jzv", all_low, dpre, preferred_element_type=F32)
    back_partial = jnp.einsum("yha,ywa->yhw", dpre, up_slices, preferred_element_type=F32)
    back = lax.psum_scatter(back_partial, "member", scatter_dimension=0, tiled=True)[0].astype(BF)
    up = lax.all_to_all(lax.psum(up_partial, "fsdp"), "member", split_axis=0, concat_axis=2, tiled=True)
    down = lax.psum(dot(normed, back, ((0,), (0,))), "fsdp")
    return (down[None], up)


def solution(mesh):
    in_specs = (
        P("member", "fsdp", None),
        P(),
        P("fsdp", "member"),
        P("member", "fsdp"),
        P("member", None, None),
        P("member", None, None),
        P("member", "fsdp"),
        P("member", "fsdp", None),
    )
    out_specs = (P("member", None, None), P("member", None, None))
    paired = mesh.shape["fsdp"] == 8 and mesh.shape["member"] == 4
    return jax.shard_map(
        paired_halves if paired else gathered,
        mesh=mesh,
        in_specs=in_specs,
        out_specs=out_specs,
        check_vma=False,
    )
```

```python
import jax
import jax.numpy as jnp
from jax import lax
from jax.experimental import pallas as pl
from jax.experimental.pallas import tpu as pltpu
from jax.sharding import PartitionSpec as P

BUCKET = 144
LMAX = 126
BF = jnp.bfloat16
F32 = jnp.float32


def normalize(frames, gain):
    values = frames.astype(F32)
    mean = jnp.mean(values, axis=1, keepdims=True)
    var = jnp.mean((values - mean) ** 2, axis=1, keepdims=True)
    return (gain * (values - mean) / jnp.sqrt(var + 1e-05)).astype(BF)


def swish_gradient(pre, dhid):
    sigma = jax.nn.sigmoid(pre)
    return (dhid * sigma * (1.0 + pre * (1.0 - sigma))).astype(BF)


def dot(a, b, dims=((1,), (0,))):
    return lax.dot_general(a, b, (dims, ((), ())), preferred_element_type=F32)


def flip(axis, size, bits):
    return lambda value: lax.ppermute(value, axis, [(i, i ^ bits) for i in range(size)])


def whole(shape):
    return pl.BlockSpec(shape, lambda: (0,) * len(shape))


def place():
    f, m = lax.axis_index("fsdp"), lax.axis_index("member")
    return f, (f >> 1) & 1, f & 1, m >> 1, m & 1


def lanes(start, size):
    return pl.ds(pl.multiple_of(start, 128), size)


def call(body, ins, outs, args, scratch=(), flops=0, size=0, vmem=40):
    return pl.pallas_call(
        body,
        in_specs=ins,
        out_specs=[whole(o.shape) for o in outs],
        out_shape=outs,
        scratch_shapes=list(scratch),
        compiler_params=pltpu.CompilerParams(vmem_limit_bytes=vmem * 1024 * 1024),
        cost_estimate=pl.CostEstimate(flops=flops, bytes_accessed=size, transcendentals=0),
    )(*args)


def prepare(frames, gain, first, turned, down_turned, up_map, lengths, cotangent, rows):
    depth, block = first.shape
    part, half = block // 4, depth // 2
    width, rank = frames.shape[2], down_turned.shape[1]
    fold = rank // 16
    lined = 2 * width + 2 * rank

    def body(frames_ref, gain_ref, first_ref, turned_ref, down_ref, up_ref, lengths_ref, cot_ref, *refs):
        own_ref, cross_ref, side_ref, same_ref, flip_ref, block_ref, masked_ref, map_ref, sems = refs
        _, low_bit, x, y, core = place()
        copies = []

        def load(src, dst):
            copy = pltpu.make_async_copy(src, dst, sems.at[len(copies)])
            copies.append(copy)
            copy.start()

        load(frames_ref.at[0, pl.ds(0, rows)], block_ref)
        load(down_ref.at[0], map_ref)
        load(cot_ref.at[0, pl.ds(0, rows)], masked_ref)
        for dl in (0, 1):
            for dx in (0, 1):
                start = ((x ^ dx) * 2 + (low_bit ^ dl)) * part
                for k in range(4):
                    src = (first_ref, turned_ref)[k // 2].at[pl.ds((k % 2) * half, half), lanes(start, part)]
                    if dx:
                        load(src, side_ref.at[pl.ds(rows, half), pl.ds((4 * dl + k) * part, part)])
                    else:
                        load(src, (same_ref, flip_ref)[dl].at[:, pl.ds(k * part, part)])
        for dc in range(2):
            start = ((1 - y) * 2 + (core ^ dc)) * block + (x * 2 + low_bit) * part
            for i in range(fold):
                load(
                    up_ref.at[0, pl.ds(16 * i, 16), lanes(start, part)],
                    cross_ref.at[pl.ds(rows, 16), pl.ds((2 * i + dc) * part, part)],
                )
        cross_ref[rows:, 2 * fold * part :] = jnp.zeros((16, lined - 2 * fold * part), BF)
        side_ref[rows:, 8 * part :] = jnp.zeros((half, lined - 8 * part), BF)
        copies[0].wait()
        normed = normalize(block_ref[...], gain_ref[...])
        for ref in (own_ref, cross_ref, side_ref):
            ref[:rows, :width] = normed
        copies[1].wait()
        low = dot(normed, map_ref[...], ((1,), (1,)))
        low = jnp.concatenate([low, jnp.zeros_like(low)], axis=1).astype(BF)
        copies[2].wait()
        keep = lax.broadcasted_iota(jnp.int32, (rows, width), 0) < lengths_ref[0, 0]
        masked = jnp.where(keep, masked_ref[...].astype(F32), 0.0).astype(BF)
        for ref in (own_ref, cross_ref, side_ref):
            ref[:rows, width : 2 * width] = masked
            ref[:rows, 2 * width :] = low
        for copy in copies[3:]:
            copy.wait()

    args = (frames, gain, first, turned, down_turned, up_map, lengths, cotangent)
    ins = [pl.BlockSpec(memory_space=pltpu.HBM)] * 8
    ins[1] = whole((width,))
    ins[6] = pl.BlockSpec(memory_space=pltpu.SMEM)
    piece = (half, 4 * part)
    shapes = [(rows, lined), (rows + 16, lined), (rows + half, lined), piece, piece]
    outs = [jax.ShapeDtypeStruct(shape, BF) for shape in shapes]
    scratch = [
        pltpu.VMEM((rows, width), BF),
        pltpu.VMEM((rows, width), BF),
        pltpu.VMEM((rank, width), BF),
        pltpu.SemaphoreType.DMA((19 + 2 * fold,)),
    ]
    return call(body, ins, outs, args, scratch, vmem=62)


def work(weights, frames, up, width, rank, own):
    if own:
        pieces, swapped = weights
        depth, part = pieces[0].shape[0] * 2, pieces[0].shape[1] // 4
    else:
        pieces, swapped = [], []
        depth, part = weights[0].shape[0] // 8, weights[0].shape[1] // 2
    rows, lined = frames[2].shape
    codes = (0, 1, 4, 6, 2, 5, 3, 7)
    n_pieces, n_swapped = len(pieces), len(swapped)
    hidden = 2 * part
    count = 4 * rows

    def body(*refs):
        piece_refs, refs = refs[:n_pieces], refs[n_pieces:]
        swap_refs, refs = refs[:n_swapped], refs[n_swapped:]
        if own:
            *frame_refs, up_ref, up_out, back_out, w_in, w_out, packed, map_ref, sems, frame_sems = refs
        else:
            w_in, w_out, *frame_refs, up_ref, out_ref, packed, map_ref, frame_sems = refs
        f, low_bit, x, y, core = place()
        slot = low_bit * 2 + x
        copies = []
        for i, ref in enumerate(frame_refs):
            at = pl.multiple_of((slot ^ i) * rows, 16)
            copies.append(
                pltpu.make_async_copy(ref.at[pl.ds(0, rows)], packed.at[pl.ds(at, rows)], frame_sems.at[i])
            )
        flat = []
        for ref in swap_refs:
            flat += [ref.at[j] for j in range(ref.shape[0])] if len(ref.shape) == 3 else [ref]
        for side, group in enumerate((piece_refs, flat)):
            for i, ref in enumerate(group):
                at = pl.multiple_of((f ^ codes[i]) * depth, 16)
                for k in range(4):
                    copies.append(
                        pltpu.make_async_copy(
                            ref.at[:, pl.ds(k * part, part)],
                            (w_in, w_out)[k // 2].at[
                                pl.ds(at + (k % 2) * (depth // 2), depth // 2), pl.ds(side * part, part)
                            ],
                            sems.at[len(copies) - 4],
                        )
                    )
        for copy in copies:
            copy.start()
        if own:
            for dc in range(2):
                start = (y * 2 + (core ^ dc)) * (4 * part) + (x * 2 + low_bit) * part
                map_ref[:, dc * part : (dc + 1) * part] = up_ref[0, :, lanes(start, part)]
        else:
            for i in range(rank // 16):
                map_ref[16 * i : 16 * (i + 1), :] = up_ref[rows:, i * hidden : (i + 1) * hidden]
        for copy in copies:
            copy.wait()
        step = 256 if hidden % 256 == 0 else part
        back = jnp.zeros((rank, count), F32)
        low = packed[:, 2 * width :][:, :rank]
        for at in range(0, hidden, step):
            now = slice(at, at + step)
            pre = dot(packed[:, :width], w_in[:, now]) + dot(low, map_ref[:, now])
            dhid = 0.5 * dot(packed[:, width : 2 * width], w_out[:, now])
            dpre = swish_gradient(pre, dhid)
            sums = dot(low, dpre, ((0,), (0,))).astype(BF)
            if own:
                up_out[:, now] = sums
            else:
                out_ref[:, now] = sums
            back = back + dot(map_ref[:, now], dpre, ((1,), (1,)))
        if own:
            back_out[...] = back
        else:
            out_ref[:, hidden:] = back.astype(BF)

    anywhere = pl.BlockSpec(memory_space=pl.ANY)
    scratch = [pltpu.VMEM((count, lined), BF), pltpu.VMEM((rank, hidden), BF)]
    whole_weights = jax.ShapeDtypeStruct((8 * depth, hidden), BF)
    if own:
        args = (*pieces, *swapped, *frames, up)
        ins = [anywhere] * (len(args) - 1) + [whole(up.shape)]
        outs = [
            jax.ShapeDtypeStruct((rank, hidden), BF),
            jax.ShapeDtypeStruct((rank, count), F32),
            whole_weights,
            whole_weights,
        ]
        scratch.append(pltpu.SemaphoreType.DMA((64,)))
    else:
        args = (*weights, *frames, up)
        ins = [whole(w.shape) for w in weights] + [anywhere] * 4 + [whole(up.shape)]
        outs = [jax.ShapeDtypeStruct((rank, hidden + count), BF)]
    scratch.append(pltpu.SemaphoreType.DMA((4,)))
    return call(body, ins, outs, args, scratch)


def down_quarter(backs, frames, width):
    rank, count = backs[0].shape
    rows, quarter = count // 4, width // 4

    def body(*refs):
        back_refs, frame_refs, (out_ref, normed, sems) = refs[:4], refs[4:8], refs[8:]
        _, low_bit, x, _, _ = place()
        slot = low_bit * 2 + x
        copies = []
        for i, ref in enumerate(frame_refs):
            copies.append(
                pltpu.make_async_copy(
                    ref.at[pl.ds(0, rows), lanes(slot * quarter, quarter)],
                    normed.at[pl.ds(pl.multiple_of((slot ^ i) * rows, 16), rows)],
                    sems.at[i],
                )
            )
        for copy in copies:
            copy.start()
        b, bx, bz, bzx = [ref[...].astype(F32) for ref in back_refs]
        back = ((b + bx) + (bz + bzx)).astype(BF)
        for copy in copies:
            copy.wait()
        out_ref[...] = dot(back, normed[...]).astype(BF)

    args = (*backs, *frames)
    ins = [whole(b.shape) for b in backs] + [pl.BlockSpec(memory_space=pl.ANY)] * 4
    scratch = [pltpu.VMEM((count, quarter), BF), pltpu.SemaphoreType.DMA((4,))]
    outs = [jax.ShapeDtypeStruct((rank, quarter), BF)]
    return call(body, ins, outs, args, scratch)[0]


def spread(own_parts, cross_parts, block):
    rank, hidden = own_parts[0].shape
    part = hidden // 2
    quarter = cross_parts[0].shape[1] - hidden

    def body(*refs):
        own_refs, cross_refs, (up_out, down_out) = refs[:4], refs[4:8], refs[8:]
        _, low_bit, x, y, core = place()
        for i in range(4):
            at = ((x * 2 + low_bit) ^ ((i & 1) * 2 + (i >> 1))) * part
            for dy, ref in enumerate((own_refs[i], cross_refs[i])):
                for dc in range(2):
                    start = ((y ^ dy) * 2 + (core ^ dc)) * block + at
                    up_out[0, :, lanes(start, part)] = ref[:, dc * part : (dc + 1) * part].astype(F32)
            at = ((low_bit * 2 + x) ^ i) * quarter
            down_out[0, :, lanes(at, quarter)] = cross_refs[i][:, hidden:].astype(F32)

    args = (*own_parts, *cross_parts)
    outs = [
        jax.ShapeDtypeStruct((1, rank, 4 * block), F32),
        jax.ShapeDtypeStruct((1, rank, 4 * quarter), F32),
    ]
    return call(body, [whole(a.shape) for a in args], outs, args)


def after(value, *done):
    return lax.optimization_barrier((value, *done))[0]


def plus(a, b):
    return (a.astype(F32) + b.astype(F32)).astype(BF)


def paired_halves(frames, gain, first, second, down_map, up_map, lengths, cotangent):
    over_x, over_low = flip("fsdp", 8, 1), flip("fsdp", 8, 2)
    over_half, over_both = flip("fsdp", 8, 4), flip("fsdp", 8, 6)
    over_xlow = flip("fsdp", 8, 3)
    over_y, over_core = flip("member", 4, 2), flip("member", 4, 1)

    width, rank = frames.shape[2], down_map.shape[2]
    rows = -(-LMAX // 16) * 16
    block = first.shape[1]
    part = block // 4
    hidden = 2 * part

    own, cross, side, w00, w01 = prepare(
        frames, gain, first, second.T, down_map.transpose(0, 2, 1), up_map, lengths, cotangent, rows
    )
    fx, fy, fz = over_x(side), over_y(cross), over_low(own)
    z2n, z3n = over_half(w00), over_both(w01)
    one = (fx, fy, fz, z2n, z3n)
    wx0, wx1 = fx[rows:, : 4 * part], fx[rows:, 4 * part : 8 * part]
    fzx, fzy = over_x(after(fz, *one)), over_y(after(fz, *one))
    z1n, z2f = over_low(after(w01, *one)), over_half(after(wx0, *one))
    near = over_core(jnp.stack([w00, wx0, z2n, z3n]))
    two = (fzx, fzy, z1n, z2f)
    fzxy, fxy = over_x(after(fzy, *two)), over_y(after(fx[:rows], *two))
    z1f, z3f = over_low(after(wx1, *two)), over_both(after(wx1, *two))
    middle = over_core(jnp.stack([z1n, z2f]))
    far = over_core(jnp.stack([z1f, z3f]))
    weights = ([w00, wx0, z2n, z3n, z1n, z2f, z1f, z3f], [near, middle, far])

    up, back, w_in, w_out = work(weights, [own, fx, fz, fzx], up_map, width, rank, True)
    (theirs,) = work((w_in, w_out), [fy, fxy, fzy, fzxy], fy, width, rank, False)

    up = plus(up, over_half(up))
    got = over_y(theirs)
    back = (back + got[:, hidden:].astype(F32)).astype(BF)
    backs = [back, over_x(back), over_low(back), over_xlow(back)]
    cross_up = got[:, :hidden]
    cross_up = plus(cross_up, over_half(cross_up))
    ups = [up, over_x(up), over_low(up), over_xlow(up)]
    down = down_quarter(backs, [own, fx, fz, fzx], width)
    down = plus(down, over_half(down))
    cross_up = jnp.concatenate([cross_up, down], axis=1)
    crosses = [cross_up, over_x(cross_up), over_low(cross_up), over_xlow(cross_up)]
    up_gradient, down_gradient = spread(ups, crosses, block)
    return (down_gradient.transpose(0, 2, 1), up_gradient)


def gathered(frames, gain, first, second, down_map, up_map, lengths, cotangent):
    members = lax.axis_size("member")
    normed = normalize(frames[0], gain)
    low = dot(normed, down_map[0]).astype(BF)
    positions = jnp.arange(BUCKET, dtype=jnp.int32)
    mask = (positions[None, :] < lengths[0][:, None]).reshape(-1)
    masked = cotangent[0] * mask.astype(BF)[:, None]
    rows = normed.shape[0]
    up_slices = lax.all_to_all(up_map, "member", split_axis=2, concat_axis=0, tiled=True)
    all_normed = lax.all_gather(normed, "member", axis=0, tiled=True)
    all_low = lax.all_gather(low, "member", axis=0, tiled=True).reshape(members, rows, -1)
    all_masked = lax.all_gather(masked, "member", axis=0, tiled=True)
    term = jnp.einsum("dgs,dsb->dgb", all_low, up_slices, preferred_element_type=F32)
    pre = term.reshape(members * rows, -1) + dot(
        all_normed, lax.all_gather(first, "fsdp", axis=0, tiled=True)
    )
    dhid = 0.5 * dot(all_masked, lax.all_gather(second, "fsdp", axis=1, tiled=True), ((1,), (1,)))
    dpre = swish_gradient(pre, dhid).reshape(members, rows, -1)
    up_partial = jnp.einsum("jnz,jnv->jzv", all_low, dpre, preferred_element_type=F32)
    back_partial = jnp.einsum("yha,ywa->yhw", dpre, up_slices, preferred_element_type=F32)
    back = lax.psum_scatter(back_partial, "member", scatter_dimension=0, tiled=True)[0].astype(BF)
    up = lax.all_to_all(lax.psum(up_partial, "fsdp"), "member", split_axis=0, concat_axis=2, tiled=True)
    down = lax.psum(dot(normed, back, ((0,), (0,))), "fsdp")
    return (down[None], up)


def solution(mesh):
    in_specs = (
        P("member", "fsdp", None),
        P(),
        P("fsdp", "member"),
        P("member", "fsdp"),
        P("member", None, None),
        P("member", None, None),
        P("member", "fsdp"),
        P("member", "fsdp", None),
    )
    out_specs = (P("member", None, None), P("member", None, None))
    paired = mesh.shape["fsdp"] == 8 and mesh.shape["member"] == 4
    return jax.shard_map(
        paired_halves if paired else gathered,
        mesh=mesh,
        in_specs=in_specs,
        out_specs=out_specs,
        check_vma=False,
    )
```

```python
import jax
import jax.numpy as jnp
from jax import lax
from jax.experimental import pallas as pl
from jax.experimental.pallas import tpu as pltpu
from jax.sharding import PartitionSpec as P

BUCKET = 144
LMAX = 126
BF = jnp.bfloat16
F32 = jnp.float32


def normalize(frames, gain):
    values = frames.astype(F32)
    mean = jnp.mean(values, axis=1, keepdims=True)
    var = jnp.mean((values - mean) ** 2, axis=1, keepdims=True)
    return (gain * (values - mean) / jnp.sqrt(var + 1e-05)).astype(BF)


def swish_gradient(pre, dhid):
    sigma = jax.nn.sigmoid(pre)
    return (dhid * sigma * (1.0 + pre * (1.0 - sigma))).astype(BF)


def dot(a, b, dims=((1,), (0,))):
    return lax.dot_general(a, b, (dims, ((), ())), preferred_element_type=F32)


def flip(axis, size, bits):
    return lambda value: lax.ppermute(value, axis, [(i, i ^ bits) for i in range(size)])


def whole(shape):
    return pl.BlockSpec(shape, lambda: (0,) * len(shape))


def place():
    f, m = lax.axis_index("fsdp"), lax.axis_index("member")
    return f, (f >> 1) & 1, f & 1, m >> 1, m & 1


def lanes(start, size):
    return pl.ds(pl.multiple_of(start, 128), size)


def call(body, ins, outs, args, scratch=(), flops=0, size=0, vmem=40):
    return pl.pallas_call(
        body,
        in_specs=ins,
        out_specs=[whole(o.shape) for o in outs],
        out_shape=outs,
        scratch_shapes=list(scratch),
        compiler_params=pltpu.CompilerParams(vmem_limit_bytes=vmem * 1024 * 1024),
        cost_estimate=pl.CostEstimate(flops=flops, bytes_accessed=size, transcendentals=0),
    )(*args)


def prepare(frames, gain, first, turned, down_turned, up_map, lengths, cotangent, rows):
    depth, block = first.shape
    part, half = block // 4, depth // 2
    width, rank = frames.shape[2], down_turned.shape[1]
    fold = rank // 16
    lined = 2 * width + 2 * rank

    def body(frames_ref, gain_ref, first_ref, turned_ref, down_ref, up_ref, lengths_ref, cot_ref, *refs):
        own_ref, cross_ref, side_ref, same_ref, flip_ref, block_ref, masked_ref, map_ref, sems = refs
        _, low_bit, x, y, core = place()
        copies = []

        def load(src, dst):
            copy = pltpu.make_async_copy(src, dst, sems.at[len(copies)])
            copies.append(copy)
            copy.start()

        load(frames_ref.at[0, pl.ds(0, rows)], block_ref)
        load(down_ref.at[0], map_ref)
        load(cot_ref.at[0, pl.ds(0, rows)], masked_ref)
        for dl in (0, 1):
            for dx in (0, 1):
                start = ((x ^ dx) * 2 + (low_bit ^ dl)) * part
                for k in range(4):
                    src = (first_ref, turned_ref)[k // 2].at[pl.ds((k % 2) * half, half), lanes(start, part)]
                    if dx:
                        load(src, side_ref.at[pl.ds(rows, half), pl.ds((4 * dl + k) * part, part)])
                    else:
                        load(src, (same_ref, flip_ref)[dl].at[:, pl.ds(k * part, part)])
        for dc in range(2):
            start = ((1 - y) * 2 + (core ^ dc)) * block + (x * 2 + low_bit) * part
            for i in range(fold):
                load(
                    up_ref.at[0, pl.ds(16 * i, 16), lanes(start, part)],
                    cross_ref.at[pl.ds(rows, 16), pl.ds((2 * i + dc) * part, part)],
                )
        cross_ref[rows:, 2 * fold * part :] = jnp.zeros((16, lined - 2 * fold * part), BF)
        side_ref[rows:, 8 * part :] = jnp.zeros((half, lined - 8 * part), BF)
        copies[0].wait()
        normed = normalize(block_ref[...], gain_ref[...])
        for ref in (own_ref, cross_ref, side_ref):
            ref[:rows, :width] = normed
        copies[1].wait()
        low = dot(normed, map_ref[...], ((1,), (1,)))
        low = jnp.concatenate([low, jnp.zeros_like(low)], axis=1).astype(BF)
        copies[2].wait()
        keep = lax.broadcasted_iota(jnp.int32, (rows, width), 0) < lengths_ref[0, 0]
        masked = jnp.where(keep, masked_ref[...].astype(F32), 0.0).astype(BF)
        for ref in (own_ref, cross_ref, side_ref):
            ref[:rows, width : 2 * width] = masked
            ref[:rows, 2 * width :] = low
        for copy in copies[3:]:
            copy.wait()

    args = (frames, gain, first, turned, down_turned, up_map, lengths, cotangent)
    ins = [pl.BlockSpec(memory_space=pltpu.HBM)] * 8
    ins[1] = whole((width,))
    ins[6] = pl.BlockSpec(memory_space=pltpu.SMEM)
    piece = (half, 4 * part)
    shapes = [(rows, lined), (rows + 16, lined), (rows + half, lined), piece, piece]
    outs = [jax.ShapeDtypeStruct(shape, BF) for shape in shapes]
    scratch = [
        pltpu.VMEM((rows, width), BF),
        pltpu.VMEM((rows, width), BF),
        pltpu.VMEM((rank, width), BF),
        pltpu.SemaphoreType.DMA((19 + 2 * fold,)),
    ]
    return call(body, ins, outs, args, scratch, vmem=62)


def work(weights, frames, up, width, rank, own):
    if own:
        pieces, swapped = weights
        depth, part = pieces[0].shape[0] * 2, pieces[0].shape[1] // 4
    else:
        pieces, swapped = [], []
        depth, part = weights[0].shape[0] // 8, weights[0].shape[1] // 2
    rows, lined = frames[2].shape
    codes = (0, 1, 4, 6, 2, 5, 3, 7)
    n_pieces, n_swapped = len(pieces), len(swapped)
    hidden = 2 * part
    count = 4 * rows
    kind = F32 if own else BF

    def body(*refs):
        piece_refs, refs = refs[:n_pieces], refs[n_pieces:]
        swap_refs, refs = refs[:n_swapped], refs[n_swapped:]
        if own:
            *frame_refs, up_ref, up_out, back_out, w_in, w_out, packed, map_ref, sems, frame_sems = refs
        else:
            w_in, w_out, *frame_refs, up_ref, up_out, back_out, packed, map_ref, frame_sems = refs
        f, low_bit, x, y, core = place()
        slot = low_bit * 2 + x
        copies = []
        for i, ref in enumerate(frame_refs):
            at = pl.multiple_of((slot ^ i) * rows, 16)
            copies.append(
                pltpu.make_async_copy(ref.at[pl.ds(0, rows)], packed.at[pl.ds(at, rows)], frame_sems.at[i])
            )
        flat = []
        for ref in swap_refs:
            flat += [ref.at[j] for j in range(ref.shape[0])] if len(ref.shape) == 3 else [ref]
        for side, group in enumerate((piece_refs, flat)):
            for i, ref in enumerate(group):
                at = pl.multiple_of((f ^ codes[i]) * depth, 16)
                for k in range(4):
                    copies.append(
                        pltpu.make_async_copy(
                            ref.at[:, pl.ds(k * part, part)],
                            (w_in, w_out)[k // 2].at[
                                pl.ds(at + (k % 2) * (depth // 2), depth // 2), pl.ds(side * part, part)
                            ],
                            sems.at[len(copies) - 4],
                        )
                    )
        for copy in copies:
            copy.start()
        if own:
            for dc in range(2):
                start = (y * 2 + (core ^ dc)) * (4 * part) + (x * 2 + low_bit) * part
                map_ref[:, dc * part : (dc + 1) * part] = up_ref[0, :, lanes(start, part)]
        else:
            for i in range(rank // 16):
                map_ref[16 * i : 16 * (i + 1), :] = up_ref[rows:, i * hidden : (i + 1) * hidden]
        for copy in copies:
            copy.wait()
        step = 256 if hidden % 256 == 0 else part
        back = jnp.zeros((rank, count), F32)
        low = packed[:, 2 * width :][:, :rank]
        for at in range(0, hidden, step):
            now = slice(at, at + step)
            pre = dot(packed[:, :width], w_in[:, now]) + dot(low, map_ref[:, now])
            dhid = 0.5 * dot(packed[:, width : 2 * width], w_out[:, now])
            dpre = swish_gradient(pre, dhid)
            up_out[:, now] = dot(low, dpre, ((0,), (0,))).astype(BF)
            back = back + dot(map_ref[:, now], dpre, ((1,), (1,)))
        back_out[...] = back.astype(kind)

    anywhere = pl.BlockSpec(memory_space=pl.ANY)
    scratch = [pltpu.VMEM((count, lined), BF), pltpu.VMEM((rank, hidden), BF)]
    whole_weights = jax.ShapeDtypeStruct((8 * depth, hidden), BF)
    if own:
        args = (*pieces, *swapped, *frames, up)
        ins = [anywhere] * (len(args) - 1) + [whole(up.shape)]
        outs = [whole_weights, whole_weights]
        scratch.append(pltpu.SemaphoreType.DMA((64,)))
    else:
        args = (*weights, *frames, up)
        ins = [whole(w.shape) for w in weights] + [anywhere] * 4 + [whole(up.shape)]
        outs = []
    sums = [jax.ShapeDtypeStruct((rank, hidden), BF), jax.ShapeDtypeStruct((rank, count), kind)]
    scratch.append(pltpu.SemaphoreType.DMA((4,)))
    return call(body, ins, sums + outs, args, scratch)


def down_half(backs, frames, width):
    rank, count = backs[0].shape
    rows, half = count // 4, width // 2
    n_backs = len(backs)

    def body(*refs):
        back_refs, frame_refs, (out_ref, normed, sems) = refs[:n_backs], refs[n_backs:-3], refs[-3:]
        _, low_bit, x, _, _ = place()
        slot = low_bit * 2 + x
        copies = []
        for i, ref in enumerate(frame_refs):
            copies.append(
                pltpu.make_async_copy(
                    ref.at[pl.ds(0, rows), lanes(x * half, half)],
                    normed.at[pl.ds(pl.multiple_of((slot ^ i) * rows, 16), rows)],
                    sems.at[i],
                )
            )
        for copy in copies:
            copy.start()
        parts = [ref[...].astype(F32) for ref in back_refs]
        while len(parts) > 1:
            parts = [parts[i] + parts[i + 1] for i in range(0, len(parts), 2)]
        back = parts[0].astype(BF)
        for copy in copies:
            copy.wait()
        out_ref[...] = dot(back, normed[...]).astype(BF)

    args = (*backs, *frames)
    ins = [whole(b.shape) for b in backs] + [pl.BlockSpec(memory_space=pl.ANY)] * 4
    scratch = [pltpu.VMEM((count, half), BF), pltpu.SemaphoreType.DMA((4,))]
    outs = [jax.ShapeDtypeStruct((rank, half), BF)]
    return call(body, ins, outs, args, scratch)[0]


def spread(ups, downs, block):
    rank, both = ups[0].shape
    part = both // 4
    half = downs[0].shape[1]

    def body(*refs):
        up_refs, down_refs, (up_out, down_out) = refs[:4], refs[4:6], refs[6:]
        _, low_bit, x, y, core = place()
        for i in range(4):
            at = ((x * 2 + low_bit) ^ ((i & 1) * 2 + (i >> 1))) * part
            for dy in range(2):
                for dc in range(2):
                    start = ((y ^ dy) * 2 + (core ^ dc)) * block + at
                    now = (2 * dy + dc) * part
                    up_out[0, :, lanes(start, part)] = up_refs[i][:, now : now + part].astype(F32)
        for i in range(2):
            down_out[0, :, lanes((x ^ i) * half, half)] = down_refs[i][...].astype(F32)

    args = (*ups, *downs)
    outs = [
        jax.ShapeDtypeStruct((1, rank, 4 * block), F32),
        jax.ShapeDtypeStruct((1, rank, 2 * half), F32),
    ]
    return call(body, [whole(a.shape) for a in args], outs, args)


def after(value, *done):
    return lax.optimization_barrier((value, *done))[0]


def plus(a, b):
    return (a.astype(F32) + b.astype(F32)).astype(BF)


def paired_halves(frames, gain, first, second, down_map, up_map, lengths, cotangent):
    over_x, over_low = flip("fsdp", 8, 1), flip("fsdp", 8, 2)
    over_half, over_both = flip("fsdp", 8, 4), flip("fsdp", 8, 6)
    over_xlow = flip("fsdp", 8, 3)
    over_y, over_core = flip("member", 4, 2), flip("member", 4, 1)
    over_yhalf = flip(("fsdp", "member"), 32, 18)

    width, rank = frames.shape[2], down_map.shape[2]
    rows = -(-LMAX // 16) * 16
    block = first.shape[1]
    part = block // 4
    hidden = 2 * part

    own, cross, side, w00, w01 = prepare(
        frames, gain, first, second.T, down_map.transpose(0, 2, 1), up_map, lengths, cotangent, rows
    )
    fx, fy, fz = over_x(side), over_y(cross), over_low(own)
    z2n, z3n = over_half(w00), over_both(w01)
    one = (fx, fy, fz, z2n, z3n)
    wx0, wx1 = fx[rows:, : 4 * part], fx[rows:, 4 * part : 8 * part]
    fzx, fzy = over_x(after(fz, *one)), over_y(after(fz, *one))
    z1n, z2f = over_low(after(w01, *one)), over_half(after(wx0, *one))
    near = over_core(jnp.stack([w00, wx0, z2n, z3n]))
    two = (fzx, fzy)
    fzxy, fxy = over_x(after(fzy, *two)), over_y(after(fx[:rows], *two))
    z1f, z3f = over_low(after(wx1, *one, z1n)), over_both(after(wx1, *one, z2f))
    middle = over_core(jnp.stack([z1n, z2f]))
    far = [over_core(z1f), over_core(z3f)]
    weights = ([w00, wx0, z2n, z3n, z1n, z2f, z1f, z3f], [near, middle, *far])

    up, back, w_in, w_out = work(weights, [own, fx, fz, fzx], up_map, width, rank, True)
    cross_up, cross_back = work((w_in, w_out), [fy, fxy, fzy, fzxy], fy, width, rank, False)

    back = (back + over_y(cross_back).astype(F32)).astype(BF)
    backs = [back, over_x(back), over_low(back), over_xlow(back)]
    cross_up = plus(over_y(cross_up), over_yhalf(cross_up))
    up = jnp.concatenate([plus(up, over_half(up)), cross_up], axis=1)
    down = down_half(backs, [own, fx, fz, fzx], width)
    down = plus(down, over_half(down))
    ups = [up, over_x(up), over_low(up), over_xlow(up)]
    downs = [down, over_x(down)]
    up_gradient, down_gradient = spread(ups, downs, block)
    return (down_gradient.transpose(0, 2, 1), up_gradient)


def gathered(frames, gain, first, second, down_map, up_map, lengths, cotangent):
    members = lax.axis_size("member")
    normed = normalize(frames[0], gain)
    low = dot(normed, down_map[0]).astype(BF)
    positions = jnp.arange(BUCKET, dtype=jnp.int32)
    mask = (positions[None, :] < lengths[0][:, None]).reshape(-1)
    masked = cotangent[0] * mask.astype(BF)[:, None]
    rows = normed.shape[0]
    up_slices = lax.all_to_all(up_map, "member", split_axis=2, concat_axis=0, tiled=True)
    all_normed = lax.all_gather(normed, "member", axis=0, tiled=True)
    all_low = lax.all_gather(low, "member", axis=0, tiled=True).reshape(members, rows, -1)
    all_masked = lax.all_gather(masked, "member", axis=0, tiled=True)
    term = jnp.einsum("dgs,dsb->dgb", all_low, up_slices, preferred_element_type=F32)
    pre = term.reshape(members * rows, -1) + dot(
        all_normed, lax.all_gather(first, "fsdp", axis=0, tiled=True)
    )
    dhid = 0.5 * dot(all_masked, lax.all_gather(second, "fsdp", axis=1, tiled=True), ((1,), (1,)))
    dpre = swish_gradient(pre, dhid).reshape(members, rows, -1)
    up_partial = jnp.einsum("jnz,jnv->jzv", all_low, dpre, preferred_element_type=F32)
    back_partial = jnp.einsum("yha,ywa->yhw", dpre, up_slices, preferred_element_type=F32)
    back = lax.psum_scatter(back_partial, "member", scatter_dimension=0, tiled=True)[0].astype(BF)
    up = lax.all_to_all(lax.psum(up_partial, "fsdp"), "member", split_axis=0, concat_axis=2, tiled=True)
    down = lax.psum(dot(normed, back, ((0,), (0,))), "fsdp")
    return (down[None], up)


def solution(mesh):
    in_specs = (
        P("member", "fsdp", None),
        P(),
        P("fsdp", "member"),
        P("member", "fsdp"),
        P("member", None, None),
        P("member", None, None),
        P("member", "fsdp"),
        P("member", "fsdp", None),
    )
    out_specs = (P("member", None, None), P("member", None, None))
    paired = mesh.shape["fsdp"] == 8 and mesh.shape["member"] == 4
    return jax.shard_map(
        paired_halves if paired else gathered,
        mesh=mesh,
        in_specs=in_specs,
        out_specs=out_specs,
        check_vma=False,
    )
```

```python
import jax
import jax.numpy as jnp
from jax import lax
from jax.experimental import pallas as pl
from jax.experimental.pallas import tpu as pltpu
from jax.sharding import PartitionSpec as P

BUCKET = 144
LMAX = 126
BF = jnp.bfloat16
F32 = jnp.float32


def normalize(frames, gain):
    values = frames.astype(F32)
    mean = jnp.mean(values, axis=1, keepdims=True)
    var = jnp.mean((values - mean) ** 2, axis=1, keepdims=True)
    return (gain * ((values - mean) * (1.0 / jnp.sqrt(var + 1e-05)))).astype(BF)


def swish_gradient(pre, dhid):
    sigma = jax.nn.sigmoid(pre)
    return (dhid * sigma * (1.0 + pre * (1.0 - sigma))).astype(BF)


def dot(a, b, dims=((1,), (0,))):
    return lax.dot_general(a, b, (dims, ((), ())), preferred_element_type=F32)


def flip(axis, size, bits):
    return lambda value: lax.ppermute(value, axis, [(i, i ^ bits) for i in range(size)])


def whole(shape):
    return pl.BlockSpec(shape, lambda: (0,) * len(shape))


def place():
    f, m = lax.axis_index("fsdp"), lax.axis_index("member")
    return f, (f >> 1) & 1, f & 1, m >> 1, m & 1


def lanes(start, size):
    return pl.ds(pl.multiple_of(start, 128), size)


def call(body, ins, outs, args, scratch=(), vmem=40, space=None):
    return pl.pallas_call(
        body,
        in_specs=ins,
        out_specs=[whole(o.shape) if space is None else pl.BlockSpec(memory_space=space) for o in outs],
        out_shape=outs,
        scratch_shapes=list(scratch),
        compiler_params=pltpu.CompilerParams(vmem_limit_bytes=vmem * 1024 * 1024),
    )(*args)


def prepare(frames, gain, first, turned, down_turned, up_map, lengths, cotangent, rows):
    depth, block = first.shape
    part, half = block // 4, depth // 2
    width, rank = frames.shape[2], down_turned.shape[1]
    fold = rank // 16
    lined = 2 * width
    below = (rows + 16, rows + 16 + rank // 2)

    def body(frames_ref, gain_ref, first_ref, turned_ref, down_ref, up_ref, lengths_ref, cot_ref, *refs):
        outs, (block_ref, masked_ref, pieces_ref, maps_ref, in_sems, out_sems) = refs[:5], refs[5:]
        own_ref, cross_ref, side_ref, same_ref, flip_ref = outs
        _, low_bit, x, y, core = place()
        loads, stores = [], []

        def load(src, dst):
            loads.append(pltpu.make_async_copy(src, dst, in_sems.at[len(loads)]))
            loads[-1].start()

        def store(src, dst):
            stores.append(pltpu.make_async_copy(src, dst, out_sems.at[len(stores)]))
            stores[-1].start()

        load(frames_ref.at[0, pl.ds(0, rows)], block_ref)
        load(cot_ref.at[0, pl.ds(0, rows)], masked_ref)
        for dx in (0, 1):
            for dl in (0, 1):
                start = ((x ^ dx) * 2 + (low_bit ^ dl)) * part
                for k in range(4):
                    src = (first_ref, turned_ref)[k // 2].at[pl.ds((k % 2) * half, half), lanes(start, part)]
                    load(src, pieces_ref.at[2 * dx + dl, :, pl.ds(k * part, part)])
        for dc in range(2):
            start = ((1 - y) * 2 + (core ^ dc)) * block + (x * 2 + low_bit) * part
            for i in range(fold):
                load(
                    up_ref.at[0, pl.ds(16 * i, 16), lanes(start, part)],
                    maps_ref.at[pl.ds(0, 16), pl.ds((2 * i + dc) * part, part)],
                )
        for i in range(2):
            load(
                down_ref.at[0, pl.ds(i * (rank // 2), rank // 2)],
                maps_ref.at[pl.ds(16, rank // 2), pl.ds(i * width, width)],
            )
        loads[1].wait()
        keep = lax.broadcasted_iota(jnp.int32, (rows, width), 0) < lengths_ref[0, 0]
        masked_ref[...] = jnp.where(keep, masked_ref[...].astype(F32), 0.0).astype(BF)
        for ref in (own_ref, cross_ref, side_ref):
            store(masked_ref, ref.at[pl.ds(0, rows), pl.ds(width, width)])
        for copy in loads[2:]:
            copy.wait()
        store(pieces_ref.at[0], same_ref)
        store(pieces_ref.at[1], flip_ref)
        for dl in range(2):
            store(pieces_ref.at[2 + dl], side_ref.at[pl.ds(rows, half), pl.ds(4 * dl * part, 4 * part)])
        store(maps_ref, cross_ref.at[pl.ds(rows, 16 + rank // 2)])
        loads[0].wait()
        block_ref[...] = normalize(block_ref[...], gain_ref[...])
        for ref in (own_ref, cross_ref, side_ref):
            store(block_ref, ref.at[pl.ds(0, rows), pl.ds(0, width)])
        for copy in stores:
            copy.wait()

    args = (frames, gain, first, turned, down_turned, up_map, lengths, cotangent)
    ins = [pl.BlockSpec(memory_space=pltpu.HBM)] * 8
    ins[1] = whole((width,))
    ins[6] = pl.BlockSpec(memory_space=pltpu.SMEM)
    piece = (half, 4 * part)
    shapes = [(rows, lined), (below[1], lined), (rows + half, lined), piece, piece]
    outs = [jax.ShapeDtypeStruct(shape, BF) for shape in shapes]
    scratch = [
        pltpu.VMEM((rows, width), BF),
        pltpu.VMEM((rows, width), BF),
        pltpu.VMEM((4, *piece), BF),
        pltpu.VMEM((16 + rank // 2, lined), BF),
        pltpu.SemaphoreType.DMA((20 + 2 * fold,)),
        pltpu.SemaphoreType.DMA((11,)),
    ]
    return call(body, ins, outs, args, scratch, vmem=62, space=pltpu.HBM)


def work(weights, frames, maps, width, rank, own):
    if own:
        pieces, swapped = weights
        depth, part = pieces[0].shape[0] * 2, pieces[0].shape[1] // 4
    else:
        pieces, swapped = [], []
        depth, part = weights[0].shape[0] // 8, weights[0].shape[1] // 2
    rows = frames[2].shape[0]
    codes = (0, 1, 4, 6, 2, 5, 3, 7)
    n_pieces, n_swapped = len(pieces), len(swapped)
    hidden = 2 * part
    count = 4 * rows
    kind = F32 if own else BF

    def body(*refs):
        piece_refs, refs = refs[:n_pieces], refs[n_pieces:]
        swap_refs, refs = refs[:n_swapped], refs[n_swapped:]
        if own:
            *frame_refs, down_ref, up_ref, up_out, back_out, w_in, w_out = refs[:10]
        else:
            w_in, w_out, *frame_refs, maps_ref, up_out, back_out = refs[:9]
        normed, masked, down_map, up_map, sems = refs[-5:]
        f, low_bit, x, y, core = place()
        slot = low_bit * 2 + x
        flat = []
        for ref in swap_refs:
            flat += [ref.at[j] for j in range(ref.shape[0])] if len(ref.shape) == 3 else [ref]
        copies = []
        for k, (w, kept) in enumerate(((w_out, masked), (w_in, normed))):
            for i, ref in enumerate(frame_refs):
                at = pl.multiple_of((slot ^ i) * rows, 16)
                copies.append((ref.at[pl.ds(0, rows), pl.ds((1 - k) * width, width)], kept.at[pl.ds(at, rows)]))
            for side, group in enumerate((piece_refs, flat)):
                for i, ref in enumerate(group):
                    for lower in range(2):
                        at = pl.multiple_of((f ^ codes[i]) * depth + lower * (depth // 2), 16)
                        copies.append(
                            (
                                ref.at[:, pl.ds((2 * (1 - k) + lower) * part, part)],
                                w.at[pl.ds(at, depth // 2), pl.ds(side * part, part)],
                            )
                        )
        copies = [pltpu.make_async_copy(src, dst, sems.at[i]) for i, (src, dst) in enumerate(copies)]
        for copy in copies:
            copy.start()
        if own:
            for dc in range(2):
                start = (y * 2 + (core ^ dc)) * (4 * part) + (x * 2 + low_bit) * part
                up_map[:, dc * part : (dc + 1) * part] = up_ref[0, :, lanes(start, part)]
            down_map[...] = down_ref[0]
        else:
            for i in range(rank // 16):
                up_map[16 * i : 16 * (i + 1), :] = maps_ref[rows : rows + 16, i * hidden : (i + 1) * hidden]
            for i in range(2):
                at = i * (rank // 2)
                down_map[at : at + rank // 2, :] = maps_ref[rows + 16 :, i * width : (i + 1) * width]
        for copy in copies:
            copy.wait()
        low = dot(down_map[...], normed[...], ((1,), (1,))).astype(BF)
        pre = dot(normed[...], w_in[...]) + dot(low.T, up_map[...])
        dhid = 0.5 * dot(masked[...], w_out[...])
        dpre = swish_gradient(pre, dhid)
        up_out[...] = dot(low, dpre).astype(BF)
        back = dot(up_map[...], dpre, ((1,), (1,)))
        back_out[...] = back.astype(kind)

    anywhere = pl.BlockSpec(memory_space=pl.ANY)
    whole_weights = jax.ShapeDtypeStruct((8 * depth, hidden), BF)
    outs = [jax.ShapeDtypeStruct((rank, hidden), BF), jax.ShapeDtypeStruct((rank, count), kind)]
    if own:
        args = (*pieces, *swapped, *frames, *maps)
        ins = [anywhere] * (len(args) - 2)
        outs += [whole_weights, whole_weights]
    else:
        args = (*weights, *frames, *maps)
        ins = [whole(w.shape) for w in weights] + [anywhere] * 4
    ins += [whole(a.shape) for a in maps]
    scratch = [
        pltpu.VMEM((count, width), BF),
        pltpu.VMEM((count, width), BF),
        pltpu.VMEM((rank, width), BF),
        pltpu.VMEM((rank, hidden), BF),
        pltpu.SemaphoreType.DMA((72 if own else 8,)),
    ]
    return call(body, ins, outs, args, scratch)


def down_half(backs, frames, width):
    rank, count = backs[0].shape
    rows, half = count // 4, width // 2
    n_backs = len(backs)

    def body(*refs):
        back_refs, frame_refs, (out_ref, normed, sems) = refs[:n_backs], refs[n_backs:-3], refs[-3:]
        _, low_bit, x, _, _ = place()
        slot = low_bit * 2 + x
        copies = []
        for i, ref in enumerate(frame_refs):
            copies.append(
                pltpu.make_async_copy(
                    ref.at[pl.ds(0, rows), lanes(x * half, half)],
                    normed.at[pl.ds(pl.multiple_of((slot ^ i) * rows, 16), rows)],
                    sems.at[i],
                )
            )
        for copy in copies:
            copy.start()
        parts = [ref[...].astype(F32) for ref in back_refs]
        while len(parts) > 1:
            parts = [parts[i] + parts[i + 1] for i in range(0, len(parts), 2)]
        back = parts[0].astype(BF)
        for copy in copies:
            copy.wait()
        out_ref[...] = dot(back, normed[...]).astype(BF)

    args = (*backs, *frames)
    ins = [whole(b.shape) for b in backs] + [pl.BlockSpec(memory_space=pl.ANY)] * 4
    scratch = [pltpu.VMEM((count, half), BF), pltpu.SemaphoreType.DMA((4,))]
    outs = [jax.ShapeDtypeStruct((rank, half), BF)]
    return call(body, ins, outs, args, scratch)[0]


def spread(ups, downs, block):
    rank, both = ups[0].shape
    part = both // 4
    half = downs[0].shape[1]

    def body(*refs):
        up_refs, down_refs, (up_out, down_out) = refs[:4], refs[4:6], refs[6:]
        _, low_bit, x, y, core = place()
        for i in range(4):
            at = ((x * 2 + low_bit) ^ ((i & 1) * 2 + (i >> 1))) * part
            for dy in range(2):
                for dc in range(2):
                    start = ((y ^ dy) * 2 + (core ^ dc)) * block + at
                    now = (2 * dy + dc) * part
                    up_out[0, :, lanes(start, part)] = up_refs[i][:, now : now + part].astype(F32)
        for i in range(2):
            down_out[0, :, lanes((x ^ i) * half, half)] = down_refs[i][...].astype(F32)

    args = (*ups, *downs)
    outs = [
        jax.ShapeDtypeStruct((1, rank, 4 * block), F32),
        jax.ShapeDtypeStruct((1, rank, 2 * half), F32),
    ]
    return call(body, [whole(a.shape) for a in args], outs, args)


def after(value, *done):
    return lax.optimization_barrier((value, *done))[0]


def plus(a, b):
    return (a.astype(F32) + b.astype(F32)).astype(BF)


def paired_halves(frames, gain, first, second, down_map, up_map, lengths, cotangent):
    over_x, over_low = flip("fsdp", 8, 1), flip("fsdp", 8, 2)
    over_half, over_both = flip("fsdp", 8, 4), flip("fsdp", 8, 6)
    over_xlow = flip("fsdp", 8, 3)
    over_y, over_core = flip("member", 4, 2), flip("member", 4, 1)
    over_yhalf = flip(("fsdp", "member"), 32, 18)

    width, rank = frames.shape[2], down_map.shape[2]
    rows = -(-LMAX // 16) * 16
    block = first.shape[1]
    part = block // 4
    hidden = 2 * part

    down_turned = down_map.transpose(0, 2, 1)
    own, cross, side, w00, w01 = prepare(
        frames, gain, first, second.T, down_turned, up_map, lengths, cotangent, rows
    )
    fx, fy, fz = over_x(side), over_y(cross), over_low(own)
    z2n, z3n = over_half(w00), over_both(w01)
    one = (fx, fy, fz, z2n, z3n)
    wx0, wx1 = fx[rows:, : 4 * part], fx[rows:, 4 * part : 8 * part]
    fzx, fzy = over_x(after(fz, fx, fy)), over_y(after(fz, fx, fy))
    z1n, z2f = over_low(after(w01, fz)), over_half(after(wx0, z2n))
    near = over_core(jnp.stack([w00, wx0, z2n, z3n]))
    two = (fzx, fzy)
    fzxy, fxy = over_x(after(fzy, *two)), over_y(after(fx[:rows], *two))
    z1f, z3f = over_low(after(wx1, *one, z1n)), over_both(after(wx1, *one, z2f))
    middle = over_core(jnp.stack([z1n, z2f]))
    far = [over_core(z1f), over_core(z3f)]
    weights = ([w00, wx0, z2n, z3n, z1n, z2f, z1f, z3f], [near, middle, *far])

    up, back, w_in, w_out = work(weights, [own, fx, fz, fzx], (down_turned, up_map), width, rank, True)
    cross_up, cross_back = work((w_in, w_out), [fy, fxy, fzy, fzxy], (fy,), width, rank, False)

    back = (back + over_y(cross_back).astype(F32)).astype(BF)
    backs = [back, over_x(back), over_low(back), over_xlow(back)]
    cross_up = plus(over_y(cross_up), over_yhalf(cross_up))
    up = jnp.concatenate([plus(up, over_half(up)), cross_up], axis=1)
    down = down_half(backs, [own, fx, fz, fzx], width)
    down = plus(down, over_half(down))
    ups = [up, over_x(up), over_low(up), over_xlow(up)]
    downs = [down, over_x(down)]
    up_gradient, down_gradient = spread(ups, downs, block)
    return (down_gradient.transpose(0, 2, 1), up_gradient)


def gathered(frames, gain, first, second, down_map, up_map, lengths, cotangent):
    members = lax.axis_size("member")
    normed = normalize(frames[0], gain)
    low = dot(normed, down_map[0]).astype(BF)
    positions = jnp.arange(BUCKET, dtype=jnp.int32)
    mask = (positions[None, :] < lengths[0][:, None]).reshape(-1)
    masked = cotangent[0] * mask.astype(BF)[:, None]
    rows = normed.shape[0]
    up_slices = lax.all_to_all(up_map, "member", split_axis=2, concat_axis=0, tiled=True)
    all_normed = lax.all_gather(normed, "member", axis=0, tiled=True)
    all_low = lax.all_gather(low, "member", axis=0, tiled=True).reshape(members, rows, -1)
    all_masked = lax.all_gather(masked, "member", axis=0, tiled=True)
    term = jnp.einsum("dgs,dsb->dgb", all_low, up_slices, preferred_element_type=F32)
    pre = term.reshape(members * rows, -1) + dot(
        all_normed, lax.all_gather(first, "fsdp", axis=0, tiled=True)
    )
    dhid = 0.5 * dot(all_masked, lax.all_gather(second, "fsdp", axis=1, tiled=True), ((1,), (1,)))
    dpre = swish_gradient(pre, dhid).reshape(members, rows, -1)
    up_partial = jnp.einsum("jnz,jnv->jzv", all_low, dpre, preferred_element_type=F32)
    back_partial = jnp.einsum("yha,ywa->yhw", dpre, up_slices, preferred_element_type=F32)
    back = lax.psum_scatter(back_partial, "member", scatter_dimension=0, tiled=True)[0].astype(BF)
    up = lax.all_to_all(lax.psum(up_partial, "fsdp"), "member", split_axis=0, concat_axis=2, tiled=True)
    down = lax.psum(dot(normed, back, ((0,), (0,))), "fsdp")
    return (down[None], up)


def solution(mesh):
    in_specs = (
        P("member", "fsdp", None),
        P(),
        P("fsdp", "member"),
        P("member", "fsdp"),
        P("member", None, None),
        P("member", None, None),
        P("member", "fsdp"),
        P("member", "fsdp", None),
    )
    out_specs = (P("member", None, None), P("member", None, None))
    paired = mesh.shape["fsdp"] == 8 and mesh.shape["member"] == 4
    return jax.shard_map(
        paired_halves if paired else gathered,
        mesh=mesh,
        in_specs=in_specs,
        out_specs=out_specs,
        check_vma=False,
    )
```

```python
import jax
import jax.numpy as jnp
from jax import lax
from jax.experimental import pallas as pl
from jax.experimental.pallas import tpu as pltpu
from jax.sharding import PartitionSpec as P

BUCKET = 144
LMAX = 126
BF = jnp.bfloat16
F32 = jnp.float32


def normalize(frames, gain):
    values = frames.astype(F32)
    mean = jnp.mean(values, axis=1, keepdims=True)
    var = jnp.mean((values - mean) ** 2, axis=1, keepdims=True)
    return (gain * ((values - mean) * (1.0 / jnp.sqrt(var + 1e-05)))).astype(BF)


def swish_gradient(pre, dhid):
    sigma = jax.nn.sigmoid(pre)
    return (dhid * sigma * (1.0 + pre * (1.0 - sigma))).astype(BF)


def dot(a, b, dims=((1,), (0,))):
    return lax.dot_general(a, b, (dims, ((), ())), preferred_element_type=F32)


def flip(axis, size, bits):
    return lambda value: lax.ppermute(value, axis, [(i, i ^ bits) for i in range(size)])


def whole(shape):
    return pl.BlockSpec(shape, lambda: (0,) * len(shape))


def place():
    f, m = lax.axis_index("fsdp"), lax.axis_index("member")
    return f, (f >> 1) & 1, f & 1, m >> 1, m & 1


def lanes(start, size):
    return pl.ds(pl.multiple_of(start, 128), size)


def call(body, ins, outs, args, scratch=(), vmem=40, space=None):
    return pl.pallas_call(
        body,
        in_specs=ins,
        out_specs=[whole(o.shape) if space is None else pl.BlockSpec(memory_space=space) for o in outs],
        out_shape=outs,
        scratch_shapes=list(scratch),
        compiler_params=pltpu.CompilerParams(vmem_limit_bytes=vmem * 1024 * 1024),
    )(*args)


def prepare(frames, gain, first, turned, down_turned, up_map, lengths, cotangent, rows):
    depth, block = first.shape
    part, half = block // 4, depth // 2
    width, rank = frames.shape[2], down_turned.shape[1]
    fold = rank // 16
    lined = 2 * width
    below = (rows + 16, rows + 16 + rank // 2)

    def body(frames_ref, gain_ref, first_ref, turned_ref, down_ref, up_ref, lengths_ref, cot_ref, *refs):
        outs, (block_ref, masked_ref, pieces_ref, maps_ref, in_sems, out_sems) = refs[:5], refs[5:]
        own_ref, cross_ref, side_ref, same_ref, flip_ref = outs
        _, low_bit, x, y, core = place()
        loads, stores = [], []

        def load(src, dst):
            loads.append(pltpu.make_async_copy(src, dst, in_sems.at[len(loads)]))
            loads[-1].start()

        def store(src, dst):
            stores.append(pltpu.make_async_copy(src, dst, out_sems.at[len(stores)]))
            stores[-1].start()

        load(frames_ref.at[0, pl.ds(0, rows)], block_ref)
        load(cot_ref.at[0, pl.ds(0, rows)], masked_ref)
        for dx in (0, 1):
            for dl in (0, 1):
                start = ((x ^ dx) * 2 + (low_bit ^ dl)) * part
                for k in range(4):
                    src = (first_ref, turned_ref)[k // 2].at[pl.ds((k % 2) * half, half), lanes(start, part)]
                    load(src, pieces_ref.at[2 * dx + dl, :, pl.ds(k * part, part)])
        for dc in range(2):
            start = ((1 - y) * 2 + (core ^ dc)) * block + (x * 2 + low_bit) * part
            for i in range(fold):
                load(
                    up_ref.at[0, pl.ds(16 * i, 16), lanes(start, part)],
                    maps_ref.at[pl.ds(0, 16), pl.ds((2 * i + dc) * part, part)],
                )
        for i in range(2):
            load(
                down_ref.at[0, pl.ds(i * (rank // 2), rank // 2)],
                maps_ref.at[pl.ds(16, rank // 2), pl.ds(i * width, width)],
            )
        loads[1].wait()
        keep = lax.broadcasted_iota(jnp.int32, (rows, width), 0) < lengths_ref[0, 0]
        masked_ref[...] = jnp.where(keep, masked_ref[...].astype(F32), 0.0).astype(BF)
        for ref in (own_ref, cross_ref, side_ref):
            store(masked_ref, ref.at[pl.ds(0, rows), pl.ds(width, width)])
        for copy in loads[2:]:
            copy.wait()
        store(pieces_ref.at[0], same_ref)
        store(pieces_ref.at[1], flip_ref)
        for dl in range(2):
            store(pieces_ref.at[2 + dl], side_ref.at[pl.ds(rows, half), pl.ds(4 * dl * part, 4 * part)])
        store(maps_ref, cross_ref.at[pl.ds(rows, 16 + rank // 2)])
        loads[0].wait()
        block_ref[...] = normalize(block_ref[...], gain_ref[...])
        for ref in (own_ref, cross_ref, side_ref):
            store(block_ref, ref.at[pl.ds(0, rows), pl.ds(0, width)])
        for copy in stores:
            copy.wait()

    args = (frames, gain, first, turned, down_turned, up_map, lengths, cotangent)
    ins = [pl.BlockSpec(memory_space=pltpu.HBM)] * 8
    ins[1] = whole((width,))
    ins[6] = pl.BlockSpec(memory_space=pltpu.SMEM)
    piece = (half, 4 * part)
    shapes = [(rows, lined), (below[1], lined), (rows + half, lined), piece, piece]
    outs = [jax.ShapeDtypeStruct(shape, BF) for shape in shapes]
    scratch = [
        pltpu.VMEM((rows, width), BF),
        pltpu.VMEM((rows, width), BF),
        pltpu.VMEM((4, *piece), BF),
        pltpu.VMEM((16 + rank // 2, lined), BF),
        pltpu.SemaphoreType.DMA((20 + 2 * fold,)),
        pltpu.SemaphoreType.DMA((11,)),
    ]
    return call(body, ins, outs, args, scratch, vmem=62, space=pltpu.HBM)


def work(weights, frames, maps, width, rank, own):
    if own:
        pieces, swapped = weights
        depth, part = pieces[0].shape[0] * 2, pieces[0].shape[1] // 4
    else:
        pieces, swapped = [], []
        depth, part = weights[0].shape[0] // 8, weights[0].shape[1] // 2
    rows = frames[2].shape[0]
    codes = (0, 1, 4, 6, 2, 5, 3, 7)
    n_pieces, n_swapped = len(pieces), len(swapped)
    hidden = 2 * part
    count = 4 * rows
    kind = F32 if own else BF

    def body(*refs):
        piece_refs, refs = refs[:n_pieces], refs[n_pieces:]
        swap_refs, refs = refs[:n_swapped], refs[n_swapped:]
        if own:
            *frame_refs, down_ref, up_ref, up_out, back_out, w_in, w_out = refs[:10]
        else:
            w_in, w_out, *frame_refs, maps_ref, up_out, back_out = refs[:9]
        down_map, up_map = refs[-2:]
        f, low_bit, x, y, core = place()
        slot = low_bit * 2 + x
        flat = []
        for ref in swap_refs:
            flat += [ref.at[j] for j in range(ref.shape[0])] if len(ref.shape) == 3 else [ref]
        for side, group in enumerate((piece_refs, flat)):
            for i, ref in enumerate(group):
                for k in range(4):
                    at = pl.multiple_of((f ^ codes[i]) * depth + (k % 2) * (depth // 2), 16)
                    w = (w_in, w_out)[k // 2]
                    w[pl.ds(at, depth // 2), side * part : (side + 1) * part] = ref[:, k * part : (k + 1) * part]
        if own:
            for dc in range(2):
                start = (y * 2 + (core ^ dc)) * (4 * part) + (x * 2 + low_bit) * part
                up_map[:, dc * part : (dc + 1) * part] = up_ref[0, :, lanes(start, part)]
            down_map[...] = down_ref[0]
        else:
            for i in range(rank // 16):
                up_map[16 * i : 16 * (i + 1), :] = maps_ref[rows : rows + 16, i * hidden : (i + 1) * hidden]
            for i in range(2):
                at = i * (rank // 2)
                down_map[at : at + rank // 2, :] = maps_ref[rows + 16 :, i * width : (i + 1) * width]
        normed = jnp.concatenate([ref[:rows, :width] for ref in frame_refs], axis=0)
        masked = jnp.concatenate([ref[:rows, width:] for ref in frame_refs], axis=0)
        low = dot(down_map[...], normed, ((1,), (1,))).astype(BF)
        pre = dot(normed, w_in[...]) + dot(low.T, up_map[...])
        dhid = 0.5 * dot(masked, w_out[...])
        dpre = swish_gradient(pre, dhid)
        up_out[...] = dot(low, dpre).astype(BF)
        back = dot(up_map[...], dpre, ((1,), (1,)))
        for i in range(4):
            back_out[:, lanes((slot ^ i) * rows, rows)] = back[:, i * rows : (i + 1) * rows].astype(kind)

    whole_weights = jax.ShapeDtypeStruct((8 * depth, hidden), BF)
    outs = [jax.ShapeDtypeStruct((rank, hidden), BF), jax.ShapeDtypeStruct((rank, count), kind)]
    if own:
        args = (*pieces, *swapped, *frames, *maps)
        ins = [whole(a.shape) for a in args]
        outs += [whole_weights, whole_weights]
    else:
        args = (*weights, *frames, *maps)
        ins = [whole(a.shape) for a in args]
    scratch = [
        pltpu.VMEM((rank, width), BF),
        pltpu.VMEM((rank, hidden), BF),
    ]
    return call(body, ins, outs, args, scratch)


def down_half(backs, frames, width):
    rank, count = backs[0].shape
    rows, half = count // 4, width // 2
    n_backs = len(backs)

    def body(*refs):
        back_refs, frame_refs, (out_ref, normed, sems) = refs[:n_backs], refs[n_backs:-3], refs[-3:]
        _, low_bit, x, _, _ = place()
        slot = low_bit * 2 + x
        copies = []
        for i, ref in enumerate(frame_refs):
            copies.append(
                pltpu.make_async_copy(
                    ref.at[pl.ds(0, rows), lanes(x * half, half)],
                    normed.at[pl.ds(pl.multiple_of((slot ^ i) * rows, 16), rows)],
                    sems.at[i],
                )
            )
        for copy in copies:
            copy.start()
        parts = [ref[...].astype(F32) for ref in back_refs]
        while len(parts) > 1:
            parts = [parts[i] + parts[i + 1] for i in range(0, len(parts), 2)]
        back = parts[0].astype(BF)
        for copy in copies:
            copy.wait()
        out_ref[...] = dot(back, normed[...]).astype(BF)

    args = (*backs, *frames)
    ins = [whole(b.shape) for b in backs] + [pl.BlockSpec(memory_space=pl.ANY)] * 4
    scratch = [pltpu.VMEM((count, half), BF), pltpu.SemaphoreType.DMA((4,))]
    outs = [jax.ShapeDtypeStruct((rank, half), BF)]
    return call(body, ins, outs, args, scratch)[0]


def spread(ups, downs, block):
    rank, both = ups[0].shape
    part = both // 4
    half = downs[0].shape[1]

    def body(*refs):
        up_refs, down_refs, (up_out, down_out) = refs[:4], refs[4:6], refs[6:]
        _, low_bit, x, y, core = place()
        for i in range(4):
            at = ((x * 2 + low_bit) ^ ((i & 1) * 2 + (i >> 1))) * part
            for dy in range(2):
                for dc in range(2):
                    start = ((y ^ dy) * 2 + (core ^ dc)) * block + at
                    now = (2 * dy + dc) * part
                    up_out[0, :, lanes(start, part)] = up_refs[i][:, now : now + part].astype(F32)
        for i in range(2):
            down_out[0, :, lanes((x ^ i) * half, half)] = down_refs[i][...].astype(F32)

    args = (*ups, *downs)
    outs = [
        jax.ShapeDtypeStruct((1, rank, 4 * block), F32),
        jax.ShapeDtypeStruct((1, rank, 2 * half), F32),
    ]
    return call(body, [whole(a.shape) for a in args], outs, args)


def after(value, *done):
    return lax.optimization_barrier((value, *done))[0]


def plus(a, b):
    return (a.astype(F32) + b.astype(F32)).astype(BF)


def paired_halves(frames, gain, first, second, down_map, up_map, lengths, cotangent):
    over_x, over_low = flip("fsdp", 8, 1), flip("fsdp", 8, 2)
    over_half, over_both = flip("fsdp", 8, 4), flip("fsdp", 8, 6)
    over_xlow = flip("fsdp", 8, 3)
    over_y, over_core = flip("member", 4, 2), flip("member", 4, 1)
    over_yhalf = flip(("fsdp", "member"), 32, 18)

    width, rank = frames.shape[2], down_map.shape[2]
    rows = -(-LMAX // 16) * 16
    block = first.shape[1]
    part = block // 4
    hidden = 2 * part

    down_turned = down_map.transpose(0, 2, 1)
    own, cross, side, w00, w01 = prepare(
        frames, gain, first, second.T, down_turned, up_map, lengths, cotangent, rows
    )
    fx, fy, fz = over_x(side), over_y(cross), over_low(own)
    z2n, z3n = over_half(w00), over_both(w01)
    one = (fx, fy, fz, z2n, z3n)
    wx0, wx1 = fx[rows:, : 4 * part], fx[rows:, 4 * part : 8 * part]
    fzx, fzy = over_x(after(fz, fx, fy)), over_y(after(fz, fx, fy))
    z1n, z2f = over_low(after(w01, fz)), over_half(after(wx0, z2n))
    near = over_core(jnp.stack([w00, wx0, z2n, z3n]))
    two = (fzx, fzy)
    fzxy, fxy = over_x(after(fzy, *two)), over_y(after(fx[:rows], *two))
    z1f, z3f = over_low(after(wx1, *one, z1n)), over_both(after(wx1, *one, z2f))
    middle = over_core(jnp.stack([z1n, z2f]))
    far = [over_core(z1f), over_core(z3f)]
    weights = ([w00, wx0, z2n, z3n, z1n, z2f, z1f, z3f], [near, middle, *far])

    up, back, w_in, w_out = work(weights, [own, fx, fz, fzx], (down_turned, up_map), width, rank, True)
    cross_up, cross_back = work((w_in, w_out), [fy, fxy, fzy, fzxy], (fy,), width, rank, False)

    back = (back + over_y(cross_back).astype(F32)).astype(BF)
    backs = [back, over_x(back), over_low(back), over_xlow(back)]
    cross_up = plus(over_y(cross_up), over_yhalf(cross_up))
    up = jnp.concatenate([plus(up, over_half(up)), cross_up], axis=1)
    down = down_half(backs, [own, fx, fz, fzx], width)
    down = plus(down, over_half(down))
    ups = [up, over_x(up), over_low(up), over_xlow(up)]
    downs = [down, over_x(down)]
    up_gradient, down_gradient = spread(ups, downs, block)
    return (down_gradient.transpose(0, 2, 1), up_gradient)


def gathered(frames, gain, first, second, down_map, up_map, lengths, cotangent):
    members = lax.axis_size("member")
    normed = normalize(frames[0], gain)
    low = dot(normed, down_map[0]).astype(BF)
    positions = jnp.arange(BUCKET, dtype=jnp.int32)
    mask = (positions[None, :] < lengths[0][:, None]).reshape(-1)
    masked = cotangent[0] * mask.astype(BF)[:, None]
    rows = normed.shape[0]
    up_slices = lax.all_to_all(up_map, "member", split_axis=2, concat_axis=0, tiled=True)
    all_normed = lax.all_gather(normed, "member", axis=0, tiled=True)
    all_low = lax.all_gather(low, "member", axis=0, tiled=True).reshape(members, rows, -1)
    all_masked = lax.all_gather(masked, "member", axis=0, tiled=True)
    term = jnp.einsum("dgs,dsb->dgb", all_low, up_slices, preferred_element_type=F32)
    pre = term.reshape(members * rows, -1) + dot(
        all_normed, lax.all_gather(first, "fsdp", axis=0, tiled=True)
    )
    dhid = 0.5 * dot(all_masked, lax.all_gather(second, "fsdp", axis=1, tiled=True), ((1,), (1,)))
    dpre = swish_gradient(pre, dhid).reshape(members, rows, -1)
    up_partial = jnp.einsum("jnz,jnv->jzv", all_low, dpre, preferred_element_type=F32)
    back_partial = jnp.einsum("yha,ywa->yhw", dpre, up_slices, preferred_element_type=F32)
    back = lax.psum_scatter(back_partial, "member", scatter_dimension=0, tiled=True)[0].astype(BF)
    up = lax.all_to_all(lax.psum(up_partial, "fsdp"), "member", split_axis=0, concat_axis=2, tiled=True)
    down = lax.psum(dot(normed, back, ((0,), (0,))), "fsdp")
    return (down[None], up)


def solution(mesh):
    in_specs = (
        P("member", "fsdp", None),
        P(),
        P("fsdp", "member"),
        P("member", "fsdp"),
        P("member", None, None),
        P("member", None, None),
        P("member", "fsdp"),
        P("member", "fsdp", None),
    )
    out_specs = (P("member", None, None), P("member", None, None))
    paired = mesh.shape["fsdp"] == 8 and mesh.shape["member"] == 4
    return jax.shard_map(
        paired_halves if paired else gathered,
        mesh=mesh,
        in_specs=in_specs,
        out_specs=out_specs,
        check_vma=False,
    )
```

```python
import jax
import jax.numpy as jnp
from jax import lax
from jax.experimental import pallas as pl
from jax.experimental.pallas import tpu as pltpu
from jax.sharding import PartitionSpec as P

BUCKET = 144
LMAX = 126
BF = jnp.bfloat16
F32 = jnp.float32


def normalize(frames, gain):
    values = frames.astype(F32)
    mean = jnp.mean(values, axis=1, keepdims=True)
    var = jnp.mean((values - mean) ** 2, axis=1, keepdims=True)
    return (gain * ((values - mean) * (1.0 / jnp.sqrt(var + 1e-05)))).astype(BF)


def swish_gradient(pre, dhid):
    sigma = jax.nn.sigmoid(pre)
    return (dhid * sigma * (1.0 + pre * (1.0 - sigma))).astype(BF)


def dot(a, b, dims=((1,), (0,))):
    return lax.dot_general(a, b, (dims, ((), ())), preferred_element_type=F32)


def flip(axis, size, bits):
    return lambda value: lax.ppermute(value, axis, [(i, i ^ bits) for i in range(size)])


def whole(shape):
    return pl.BlockSpec(shape, lambda: (0,) * len(shape))


def place():
    f, m = lax.axis_index("fsdp"), lax.axis_index("member")
    return f, (f >> 1) & 1, f & 1, m >> 1, m & 1


def lanes(start, size):
    return pl.ds(pl.multiple_of(start, 128), size)


def call(body, ins, outs, args, scratch=(), vmem=40, space=None):
    return pl.pallas_call(
        body,
        in_specs=ins,
        out_specs=[whole(o.shape) if space is None else pl.BlockSpec(memory_space=space) for o in outs],
        out_shape=outs,
        scratch_shapes=list(scratch),
        compiler_params=pltpu.CompilerParams(vmem_limit_bytes=vmem * 1024 * 1024),
    )(*args)


def prepare(frames, gain, first, turned, down_turned, up_map, lengths, cotangent, rows):
    depth, block = first.shape
    part, half = block // 4, depth // 2
    width, rank = frames.shape[2], down_turned.shape[1]
    fold = rank // 16
    lined = 2 * width
    below = (rows + 16, rows + 16 + rank // 2)

    def body(frames_ref, gain_ref, first_ref, turned_ref, down_ref, up_ref, lengths_ref, cot_ref, *refs):
        outs, (block_ref, masked_ref, pieces_ref, maps_ref, in_sems, out_sems) = refs[:5], refs[5:]
        own_ref, cross_ref, side_ref, same_ref, flip_ref = outs
        _, low_bit, x, y, core = place()
        loads, stores = [], []

        def load(src, dst):
            loads.append(pltpu.make_async_copy(src, dst, in_sems.at[len(loads)]))
            loads[-1].start()

        def store(src, dst):
            stores.append(pltpu.make_async_copy(src, dst, out_sems.at[len(stores)]))
            stores[-1].start()

        load(frames_ref.at[0, pl.ds(0, rows)], block_ref)
        load(cot_ref.at[0, pl.ds(0, rows)], masked_ref)
        for dx in (0, 1):
            for dl in (0, 1):
                start = ((x ^ dx) * 2 + (low_bit ^ dl)) * part
                for k in range(4):
                    src = (first_ref, turned_ref)[k // 2].at[pl.ds((k % 2) * half, half), lanes(start, part)]
                    load(src, pieces_ref.at[2 * dx + dl, :, pl.ds(k * part, part)])
        for dc in range(2):
            start = ((1 - y) * 2 + (core ^ dc)) * block + (x * 2 + low_bit) * part
            for i in range(fold):
                load(
                    up_ref.at[0, pl.ds(16 * i, 16), lanes(start, part)],
                    maps_ref.at[pl.ds(0, 16), pl.ds((2 * i + dc) * part, part)],
                )
        for i in range(2):
            load(
                down_ref.at[0, pl.ds(i * (rank // 2), rank // 2)],
                maps_ref.at[pl.ds(16, rank // 2), pl.ds(i * width, width)],
            )
        loads[1].wait()
        keep = lax.broadcasted_iota(jnp.int32, (rows, width), 0) < lengths_ref[0, 0]
        masked_ref[...] = jnp.where(keep, masked_ref[...].astype(F32), 0.0).astype(BF)
        for ref in (own_ref, cross_ref, side_ref):
            store(masked_ref, ref.at[pl.ds(0, rows), pl.ds(width, width)])
        for copy in loads[2:]:
            copy.wait()
        store(pieces_ref.at[0], same_ref)
        store(pieces_ref.at[1], flip_ref)
        for dl in range(2):
            store(pieces_ref.at[2 + dl], side_ref.at[pl.ds(rows, half), pl.ds(4 * dl * part, 4 * part)])
        store(maps_ref, cross_ref.at[pl.ds(rows, 16 + rank // 2)])
        loads[0].wait()
        block_ref[...] = normalize(block_ref[...], gain_ref[...])
        for ref in (own_ref, cross_ref, side_ref):
            store(block_ref, ref.at[pl.ds(0, rows), pl.ds(0, width)])
        for copy in stores:
            copy.wait()

    args = (frames, gain, first, turned, down_turned, up_map, lengths, cotangent)
    ins = [pl.BlockSpec(memory_space=pltpu.HBM)] * 8
    ins[1] = whole((width,))
    ins[6] = pl.BlockSpec(memory_space=pltpu.SMEM)
    piece = (half, 4 * part)
    shapes = [(rows, lined), (below[1], lined), (rows + half, lined), piece, piece]
    outs = [jax.ShapeDtypeStruct(shape, BF) for shape in shapes]
    scratch = [
        pltpu.VMEM((rows, width), BF),
        pltpu.VMEM((rows, width), BF),
        pltpu.VMEM((4, *piece), BF),
        pltpu.VMEM((16 + rank // 2, lined), BF),
        pltpu.SemaphoreType.DMA((20 + 2 * fold,)),
        pltpu.SemaphoreType.DMA((11,)),
    ]
    return call(body, ins, outs, args, scratch, vmem=62, space=pltpu.HBM)


def low_of(frames, down_turned):
    rows, rank, width = frames[0].shape[0], down_turned.shape[1], down_turned.shape[2]

    def body(*refs):
        frame_refs, (down_ref, out_ref) = refs[:4], refs[4:]
        normed = jnp.concatenate([ref[:rows, :width] for ref in frame_refs], axis=0)
        out_ref[...] = dot(down_ref[0], normed, ((1,), (1,))).astype(BF)

    args = (*frames, down_turned)
    outs = [jax.ShapeDtypeStruct((rank, 4 * rows), BF)]
    return call(body, [whole(a.shape) for a in args], outs, args)[0]


def work(weights, frames, maps, width, rank, own):
    if own:
        pieces, swapped = weights
        depth, part = pieces[0].shape[0] * 2, pieces[0].shape[1] // 4
    else:
        pieces, swapped = [], []
        depth, part = weights[0].shape[0] // 8, weights[0].shape[1] // 2
    rows = frames[2].shape[0]
    codes = (0, 1, 4, 6, 2, 5, 3, 7)
    n_pieces, n_swapped = len(pieces), len(swapped)
    hidden = 2 * part
    count = 4 * rows
    kind = F32 if own else BF

    def body(*refs):
        piece_refs, refs = refs[:n_pieces], refs[n_pieces:]
        swap_refs, refs = refs[:n_swapped], refs[n_swapped:]
        if own:
            *frame_refs, low_ref, up_ref, up_out, back_out, w_in, w_out = refs[:10]
        else:
            w_in, w_out, *frame_refs, maps_ref, up_out, back_out = refs[:9]
        down_map, up_map = refs[-2:]
        f, low_bit, x, y, core = place()
        slot = low_bit * 2 + x
        flat = []
        for ref in swap_refs:
            flat += [ref.at[j] for j in range(ref.shape[0])] if len(ref.shape) == 3 else [ref]
        for side, group in enumerate((piece_refs, flat)):
            for i, ref in enumerate(group):
                for k in range(4):
                    at = pl.multiple_of((f ^ codes[i]) * depth + (k % 2) * (depth // 2), 16)
                    w = (w_in, w_out)[k // 2]
                    w[pl.ds(at, depth // 2), side * part : (side + 1) * part] = ref[:, k * part : (k + 1) * part]
        if own:
            for dc in range(2):
                start = (y * 2 + (core ^ dc)) * (4 * part) + (x * 2 + low_bit) * part
                up_map[:, dc * part : (dc + 1) * part] = up_ref[0, :, lanes(start, part)]
        else:
            for i in range(rank // 16):
                up_map[16 * i : 16 * (i + 1), :] = maps_ref[rows : rows + 16, i * hidden : (i + 1) * hidden]
            for i in range(2):
                at = i * (rank // 2)
                down_map[at : at + rank // 2, :] = maps_ref[rows + 16 :, i * width : (i + 1) * width]
        normed = jnp.concatenate([ref[:rows, :width] for ref in frame_refs], axis=0)
        masked = jnp.concatenate([ref[:rows, width:] for ref in frame_refs], axis=0)
        low = low_ref[...] if own else dot(down_map[...], normed, ((1,), (1,))).astype(BF)
        pre = dot(normed, w_in[...]) + dot(low.T, up_map[...])
        dhid = 0.5 * dot(masked, w_out[...])
        dpre = swish_gradient(pre, dhid)
        up_out[...] = dot(low, dpre).astype(BF)
        back = dot(up_map[...], dpre, ((1,), (1,)))
        for i in range(4):
            back_out[:, lanes((slot ^ i) * rows, rows)] = back[:, i * rows : (i + 1) * rows].astype(kind)

    whole_weights = jax.ShapeDtypeStruct((8 * depth, hidden), BF)
    outs = [jax.ShapeDtypeStruct((rank, hidden), BF), jax.ShapeDtypeStruct((rank, count), kind)]
    if own:
        args = (*pieces, *swapped, *frames, *maps)
        ins = [whole(a.shape) for a in args]
        outs += [whole_weights, whole_weights]
    else:
        args = (*weights, *frames, *maps)
        ins = [whole(a.shape) for a in args]
    scratch = [
        pltpu.VMEM((rank, width), BF),
        pltpu.VMEM((rank, hidden), BF),
    ]
    return call(body, ins, outs, args, scratch)


def down_half(backs, frames, width):
    rank, count = backs[0].shape
    rows, half = count // 4, width // 2

    def body(*refs):
        back_refs, frame_refs, out_ref, normed = refs[:4], refs[4:8], refs[8], refs[9]
        _, low_bit, x, _, _ = place()
        slot = low_bit * 2 + x
        for i, ref in enumerate(frame_refs):
            at = pl.multiple_of((slot ^ i) * rows, 16)
            normed[pl.ds(at, rows), :] = ref[:rows, lanes(x * half, half)]
        b, bx, bz, bzx = [ref[...].astype(F32) for ref in back_refs]
        back = ((b + bx) + (bz + bzx)).astype(BF)
        out_ref[...] = dot(back, normed[...]).astype(BF)

    args = (*backs, *frames)
    outs = [jax.ShapeDtypeStruct((rank, half), BF)]
    return call(body, [whole(a.shape) for a in args], outs, args, [pltpu.VMEM((count, half), BF)])[0]


def spread(ups, downs, block):
    rank, both = ups[0].shape
    part = both // 4
    half = downs[0].shape[1]

    def body(*refs):
        up_refs, down_refs, (up_out, down_out) = refs[:4], refs[4:6], refs[6:]
        _, low_bit, x, y, core = place()
        for i in range(4):
            at = ((x * 2 + low_bit) ^ ((i & 1) * 2 + (i >> 1))) * part
            for dy in range(2):
                for dc in range(2):
                    start = ((y ^ dy) * 2 + (core ^ dc)) * block + at
                    now = (2 * dy + dc) * part
                    up_out[0, :, lanes(start, part)] = up_refs[i][:, now : now + part].astype(F32)
        for i in range(2):
            down_out[0, :, lanes((x ^ i) * half, half)] = down_refs[i][...].astype(F32)

    args = (*ups, *downs)
    outs = [
        jax.ShapeDtypeStruct((1, rank, 4 * block), F32),
        jax.ShapeDtypeStruct((1, rank, 2 * half), F32),
    ]
    return call(body, [whole(a.shape) for a in args], outs, args)


def after(value, *done):
    return lax.optimization_barrier((value, *done))[0]


def plus(a, b):
    return (a.astype(F32) + b.astype(F32)).astype(BF)


def paired_halves(frames, gain, first, second, down_map, up_map, lengths, cotangent):
    over_x, over_low = flip("fsdp", 8, 1), flip("fsdp", 8, 2)
    over_half, over_both = flip("fsdp", 8, 4), flip("fsdp", 8, 6)
    over_xlow = flip("fsdp", 8, 3)
    over_y, over_core = flip("member", 4, 2), flip("member", 4, 1)
    over_yhalf = flip(("fsdp", "member"), 32, 18)

    width, rank = frames.shape[2], down_map.shape[2]
    rows = -(-LMAX // 16) * 16
    block = first.shape[1]
    part = block // 4
    hidden = 2 * part

    down_turned = down_map.transpose(0, 2, 1)
    own, cross, side, w00, w01 = prepare(
        frames, gain, first, second.T, down_turned, up_map, lengths, cotangent, rows
    )
    fx, fy, fz = over_x(side), over_y(cross), over_low(own)
    z2n, z3n = over_half(w00), over_both(w01)
    one = (fx, fy, fz, z2n, z3n)
    wx0, wx1 = fx[rows:, : 4 * part], fx[rows:, 4 * part : 8 * part]
    fzx, fzy = over_x(after(fz, fx, fy)), over_y(after(fz, fx, fy))
    z1n, z2f = over_low(after(w01, fz)), over_half(after(wx0, z2n))
    near = over_core(jnp.stack([w00, wx0, z2n, z3n]))
    two = (fzx, fzy)
    fzxy, fxy = over_x(after(fzy, *two)), over_y(after(fx[:rows], *two))
    z1f, z3f = over_low(after(wx1, *one, z1n)), over_both(after(wx1, *one, z2f))
    middle = over_core(jnp.stack([z1n, z2f]))
    low = low_of([own, fx, fz, fzx], down_turned)
    far = [over_core(z1f), over_core(z3f)]
    weights = ([w00, wx0, z2n, z3n, z1n, z2f, z1f, z3f], [near, middle, *far])

    up, back, w_in, w_out = work(weights, [own, fx, fz, fzx], (low, up_map), width, rank, True)
    cross_up, cross_back = work((w_in, w_out), [fy, fxy, fzy, fzxy], (fy,), width, rank, False)

    back = (back + over_y(cross_back).astype(F32)).astype(BF)
    backs = [back, over_x(back), over_low(back), over_xlow(back)]
    cross_up = plus(over_y(cross_up), over_yhalf(cross_up))
    up = jnp.concatenate([plus(up, over_half(up)), cross_up], axis=1)
    down = down_half(backs, [own, fx, fz, fzx], width)
    down = plus(down, over_half(down))
    ups = [up, over_x(up), over_low(up), over_xlow(up)]
    downs = [down, over_x(down)]
    up_gradient, down_gradient = spread(ups, downs, block)
    return (down_gradient.transpose(0, 2, 1), up_gradient)


def gathered(frames, gain, first, second, down_map, up_map, lengths, cotangent):
    members = lax.axis_size("member")
    normed = normalize(frames[0], gain)
    low = dot(normed, down_map[0]).astype(BF)
    positions = jnp.arange(BUCKET, dtype=jnp.int32)
    mask = (positions[None, :] < lengths[0][:, None]).reshape(-1)
    masked = cotangent[0] * mask.astype(BF)[:, None]
    rows = normed.shape[0]
    up_slices = lax.all_to_all(up_map, "member", split_axis=2, concat_axis=0, tiled=True)
    all_normed = lax.all_gather(normed, "member", axis=0, tiled=True)
    all_low = lax.all_gather(low, "member", axis=0, tiled=True).reshape(members, rows, -1)
    all_masked = lax.all_gather(masked, "member", axis=0, tiled=True)
    term = jnp.einsum("dgs,dsb->dgb", all_low, up_slices, preferred_element_type=F32)
    pre = term.reshape(members * rows, -1) + dot(
        all_normed, lax.all_gather(first, "fsdp", axis=0, tiled=True)
    )
    dhid = 0.5 * dot(all_masked, lax.all_gather(second, "fsdp", axis=1, tiled=True), ((1,), (1,)))
    dpre = swish_gradient(pre, dhid).reshape(members, rows, -1)
    up_partial = jnp.einsum("jnz,jnv->jzv", all_low, dpre, preferred_element_type=F32)
    back_partial = jnp.einsum("yha,ywa->yhw", dpre, up_slices, preferred_element_type=F32)
    back = lax.psum_scatter(back_partial, "member", scatter_dimension=0, tiled=True)[0].astype(BF)
    up = lax.all_to_all(lax.psum(up_partial, "fsdp"), "member", split_axis=0, concat_axis=2, tiled=True)
    down = lax.psum(dot(normed, back, ((0,), (0,))), "fsdp")
    return (down[None], up)


def solution(mesh):
    in_specs = (
        P("member", "fsdp", None),
        P(),
        P("fsdp", "member"),
        P("member", "fsdp"),
        P("member", None, None),
        P("member", None, None),
        P("member", "fsdp"),
        P("member", "fsdp", None),
    )
    out_specs = (P("member", None, None), P("member", None, None))
    paired = mesh.shape["fsdp"] == 8 and mesh.shape["member"] == 4
    return jax.shard_map(
        paired_halves if paired else gathered,
        mesh=mesh,
        in_specs=in_specs,
        out_specs=out_specs,
        check_vma=False,
    )
```

```python
import jax
import jax.numpy as jnp
from jax import lax
from jax.experimental import pallas as pl
from jax.experimental.pallas import tpu as pltpu
from jax.sharding import PartitionSpec as P

BUCKET = 144
LMAX = 126
BF = jnp.bfloat16
F32 = jnp.float32


def normalize(frames, gain):
    values = frames.astype(F32)
    mean = jnp.mean(values, axis=1, keepdims=True)
    var = jnp.mean((values - mean) ** 2, axis=1, keepdims=True)
    return (gain * ((values - mean) * (1.0 / jnp.sqrt(var + 1e-05)))).astype(BF)


def swish_gradient(pre, dhid):
    sigma = jax.nn.sigmoid(pre)
    return (dhid * sigma * (1.0 + pre * (1.0 - sigma))).astype(BF)


def dot(a, b, dims=((1,), (0,))):
    return lax.dot_general(a, b, (dims, ((), ())), preferred_element_type=F32)


def flip(axis, size, bits):
    return lambda value: lax.ppermute(value, axis, [(i, i ^ bits) for i in range(size)])


def whole(shape):
    return pl.BlockSpec(shape, lambda: (0,) * len(shape))


def place():
    f, m = lax.axis_index("fsdp"), lax.axis_index("member")
    return f, (f >> 1) & 1, f & 1, m >> 1, m & 1


def lanes(start, size):
    return pl.ds(pl.multiple_of(start, 128), size)


def call(body, ins, outs, args, scratch=(), vmem=40, space=None):
    return pl.pallas_call(
        body,
        in_specs=ins,
        out_specs=[whole(o.shape) if space is None else pl.BlockSpec(memory_space=space) for o in outs],
        out_shape=outs,
        scratch_shapes=list(scratch),
        compiler_params=pltpu.CompilerParams(vmem_limit_bytes=vmem * 1024 * 1024),
    )(*args)


def prepare(frames, gain, first, turned, down_turned, up_map, lengths, cotangent, rows):
    depth, block = first.shape
    part, half = block // 4, depth // 2
    width, rank = frames.shape[2], down_turned.shape[1]
    fold = rank // 16
    lined = 2 * width
    below = (rows + 16, rows + 16 + rank // 2)

    def body(frames_ref, gain_ref, first_ref, turned_ref, down_ref, up_ref, lengths_ref, cot_ref, *refs):
        outs, (block_ref, masked_ref, pieces_ref, maps_ref, in_sems, out_sems) = refs[:5], refs[5:]
        own_ref, cross_ref, side_ref, same_ref, flip_ref = outs
        _, low_bit, x, y, core = place()
        loads, stores = [], []

        def load(src, dst):
            loads.append(pltpu.make_async_copy(src, dst, in_sems.at[len(loads)]))
            loads[-1].start()

        def store(src, dst):
            stores.append(pltpu.make_async_copy(src, dst, out_sems.at[len(stores)]))
            stores[-1].start()

        load(frames_ref.at[0, pl.ds(0, rows)], block_ref)
        load(cot_ref.at[0, pl.ds(0, rows)], masked_ref)
        for dx in (0, 1):
            for dl in (0, 1):
                start = ((x ^ dx) * 2 + (low_bit ^ dl)) * part
                for k in range(4):
                    src = (first_ref, turned_ref)[k // 2].at[pl.ds((k % 2) * half, half), lanes(start, part)]
                    load(src, pieces_ref.at[2 * dx + dl, :, pl.ds(k * part, part)])
        for dc in range(2):
            start = ((1 - y) * 2 + (core ^ dc)) * block + (x * 2 + low_bit) * part
            for i in range(fold):
                load(
                    up_ref.at[0, pl.ds(16 * i, 16), lanes(start, part)],
                    maps_ref.at[pl.ds(0, 16), pl.ds((2 * i + dc) * part, part)],
                )
        for i in range(2):
            load(
                down_ref.at[0, pl.ds(i * (rank // 2), rank // 2)],
                maps_ref.at[pl.ds(16, rank // 2), pl.ds(i * width, width)],
            )
        loads[1].wait()
        keep = lax.broadcasted_iota(jnp.int32, (rows, width), 0) < lengths_ref[0, 0]
        masked_ref[...] = jnp.where(keep, masked_ref[...].astype(F32), 0.0).astype(BF)
        for ref in (own_ref, cross_ref, side_ref):
            store(masked_ref, ref.at[pl.ds(0, rows), pl.ds(width, width)])
        for copy in loads[2:]:
            copy.wait()
        store(pieces_ref.at[0], same_ref)
        store(pieces_ref.at[1], flip_ref)
        for dl in range(2):
            store(pieces_ref.at[2 + dl], side_ref.at[pl.ds(rows, half), pl.ds(4 * dl * part, 4 * part)])
        store(maps_ref, cross_ref.at[pl.ds(rows, 16 + rank // 2)])
        loads[0].wait()
        block_ref[...] = normalize(block_ref[...], gain_ref[...])
        for ref in (own_ref, cross_ref, side_ref):
            store(block_ref, ref.at[pl.ds(0, rows), pl.ds(0, width)])
        for copy in stores:
            copy.wait()

    args = (frames, gain, first, turned, down_turned, up_map, lengths, cotangent)
    ins = [pl.BlockSpec(memory_space=pltpu.HBM)] * 8
    ins[1] = whole((width,))
    ins[6] = pl.BlockSpec(memory_space=pltpu.SMEM)
    piece = (half, 4 * part)
    shapes = [(rows, lined), (below[1], lined), (rows + half, lined), piece, piece]
    outs = [jax.ShapeDtypeStruct(shape, BF) for shape in shapes]
    scratch = [
        pltpu.VMEM((rows, width), BF),
        pltpu.VMEM((rows, width), BF),
        pltpu.VMEM((4, *piece), BF),
        pltpu.VMEM((16 + rank // 2, lined), BF),
        pltpu.SemaphoreType.DMA((20 + 2 * fold,)),
        pltpu.SemaphoreType.DMA((11,)),
    ]
    return call(body, ins, outs, args, scratch, vmem=62, space=pltpu.HBM)


def low_of(frames, down_turned):
    rows, rank, width = frames[0].shape[0], down_turned.shape[1], down_turned.shape[2]

    def body(*refs):
        frame_refs, (down_ref, out_ref) = refs[:4], refs[4:]
        normed = jnp.concatenate([ref[:rows, :width] for ref in frame_refs], axis=0)
        out_ref[...] = dot(down_ref[0], normed, ((1,), (1,))).astype(BF)

    args = (*frames, down_turned)
    outs = [jax.ShapeDtypeStruct((rank, 4 * rows), BF)]
    return call(body, [whole(a.shape) for a in args], outs, args)[0]


def work(weights, frames, maps, width, rank, own):
    if own:
        pieces, swapped = weights
        depth, part = pieces[0].shape[0] * 2, pieces[0].shape[1] // 4
    else:
        pieces, swapped = [], []
        depth, part = weights[0].shape[0] // 8, weights[0].shape[1] // 2
    rows = frames[2].shape[0]
    codes = (0, 1, 4, 6, 2, 5, 3, 7)
    n_pieces, n_swapped = len(pieces), len(swapped)
    hidden = 2 * part
    count = 4 * rows
    kind = F32 if own else BF

    def body(*refs):
        piece_refs, refs = refs[:n_pieces], refs[n_pieces:]
        swap_refs, refs = refs[:n_swapped], refs[n_swapped:]
        if own:
            *frame_refs, low_ref, up_ref, up_out, back_out, w_in, w_out = refs[:10]
        else:
            w_in, w_out, *frame_refs, maps_ref, up_out, back_out = refs[:9]
        down_map, up_map = refs[-2:]
        f, low_bit, x, y, core = place()
        slot = low_bit * 2 + x
        flat = []
        for ref in swap_refs:
            flat += [ref.at[j] for j in range(ref.shape[0])] if len(ref.shape) == 3 else [ref]
        for side, group in enumerate((piece_refs, flat)):
            for i, ref in enumerate(group):
                for k in range(4):
                    at = pl.multiple_of((f ^ codes[i]) * depth + (k % 2) * (depth // 2), 16)
                    w = (w_in, w_out)[k // 2]
                    w[pl.ds(at, depth // 2), side * part : (side + 1) * part] = ref[:, k * part : (k + 1) * part]
        if own:
            for dc in range(2):
                start = (y * 2 + (core ^ dc)) * (4 * part) + (x * 2 + low_bit) * part
                up_map[:, dc * part : (dc + 1) * part] = up_ref[0, :, lanes(start, part)]
        else:
            for i in range(rank // 16):
                up_map[16 * i : 16 * (i + 1), :] = maps_ref[rows : rows + 16, i * hidden : (i + 1) * hidden]
            for i in range(2):
                at = i * (rank // 2)
                down_map[at : at + rank // 2, :] = maps_ref[rows + 16 :, i * width : (i + 1) * width]
        normed = jnp.concatenate([ref[:rows, :width] for ref in frame_refs], axis=0)
        masked = jnp.concatenate([ref[:rows, width:] for ref in frame_refs], axis=0)
        low = low_ref[...] if own else dot(down_map[...], normed, ((1,), (1,))).astype(BF)
        pre = dot(normed, w_in[...]) + dot(low.T, up_map[...])
        dhid = 0.5 * dot(masked, w_out[...])
        dpre = swish_gradient(pre, dhid)
        up_out[...] = dot(low, dpre).astype(BF)
        back = dot(up_map[...], dpre, ((1,), (1,)))
        for i in range(4):
            back_out[:, lanes((slot ^ i) * rows, rows)] = back[:, i * rows : (i + 1) * rows].astype(kind)

    whole_weights = jax.ShapeDtypeStruct((8 * depth, hidden), BF)
    outs = [jax.ShapeDtypeStruct((rank, hidden), BF), jax.ShapeDtypeStruct((rank, count), kind)]
    if own:
        args = (*pieces, *swapped, *frames, *maps)
        ins = [whole(a.shape) for a in args]
        outs += [whole_weights, whole_weights]
    else:
        args = (*weights, *frames, *maps)
        ins = [whole(a.shape) for a in args]
    scratch = [
        pltpu.VMEM((rank, width), BF),
        pltpu.VMEM((rank, hidden), BF),
    ]
    return call(body, ins, outs, args, scratch)


def down_half(backs, frames, width):
    rank, count = backs[0].shape
    rows, half = count // 4, width // 2

    def body(*refs):
        back_refs, frame_refs, out_ref, normed = refs[:4], refs[4:8], refs[8], refs[9]
        _, low_bit, x, _, _ = place()
        slot = low_bit * 2 + x
        for i, ref in enumerate(frame_refs):
            at = pl.multiple_of((slot ^ i) * rows, 16)
            normed[pl.ds(at, rows), :] = ref[:rows, lanes(x * half, half)]
        b, bx, bz, bzx = [ref[...].astype(F32) for ref in back_refs]
        back = ((b + bx) + (bz + bzx)).astype(BF)
        out_ref[...] = dot(back, normed[...]).astype(BF)

    args = (*backs, *frames)
    outs = [jax.ShapeDtypeStruct((rank, half), BF)]
    return call(body, [whole(a.shape) for a in args], outs, args, [pltpu.VMEM((count, half), BF)])[0]


def spread(ups, downs, block):
    rank, both = ups[0].shape
    part = both // 4
    half = downs[0].shape[1]

    def body(*refs):
        up_refs, down_refs, (up_out, down_out) = refs[:4], refs[4:6], refs[6:]
        _, low_bit, x, y, core = place()
        for i in range(4):
            at = ((x * 2 + low_bit) ^ ((i & 1) * 2 + (i >> 1))) * part
            for dy in range(2):
                for dc in range(2):
                    start = ((y ^ dy) * 2 + (core ^ dc)) * block + at
                    now = (2 * dy + dc) * part
                    up_out[0, :, lanes(start, part)] = up_refs[i][:, now : now + part].astype(F32)
        for i in range(2):
            down_out[0, :, lanes((x ^ i) * half, half)] = down_refs[i][...].astype(F32)

    args = (*ups, *downs)
    outs = [
        jax.ShapeDtypeStruct((1, rank, 4 * block), F32),
        jax.ShapeDtypeStruct((1, rank, 2 * half), F32),
    ]
    return call(body, [whole(a.shape) for a in args], outs, args)


def after(value, *done):
    return lax.optimization_barrier((value, *done))[0]


def plus(a, b):
    return (a.astype(F32) + b.astype(F32)).astype(BF)


def paired_halves(frames, gain, first, second, down_map, up_map, lengths, cotangent):
    over_x, over_low = flip("fsdp", 8, 1), flip("fsdp", 8, 2)
    over_half, over_both = flip("fsdp", 8, 4), flip("fsdp", 8, 6)
    over_xlow = flip("fsdp", 8, 3)
    over_y, over_core = flip("member", 4, 2), flip("member", 4, 1)
    over_yhalf = flip(("fsdp", "member"), 32, 18)

    width, rank = frames.shape[2], down_map.shape[2]
    rows = -(-LMAX // 16) * 16
    block = first.shape[1]
    part = block // 4
    hidden = 2 * part

    down_turned = down_map.transpose(0, 2, 1)
    own, cross, side, w00, w01 = prepare(
        frames, gain, first, second.T, down_turned, up_map, lengths, cotangent, rows
    )
    fx, fy, fz = over_x(side), over_y(cross), over_low(own)
    z2n, z3n = over_half(w00), over_both(w01)
    one = (fx, fy, fz, z2n, z3n)
    wx0, wx1 = fx[rows:, : 4 * part], fx[rows:, 4 * part : 8 * part]
    fzx, fzy = over_x(after(fz, fx)), over_y(after(fz, fx, fy))
    z1n, z2f = over_low(after(w01, fz)), over_half(after(wx0, z2n))
    near = over_core(jnp.stack([w00, wx0, z2n, z3n]))
    two = (fzx, fzy)
    fzxy, fxy = over_x(after(fzy, *two)), over_y(after(fx[:rows], *two))
    z1f, z3f = over_low(after(wx1, *one, z1n)), over_both(after(wx1, *one, z2f))
    middle = over_core(jnp.stack([z1n, z2f]))
    low = low_of([own, fx, fz, fzx], down_turned)
    far = [over_core(z1f), over_core(z3f)]
    weights = ([w00, wx0, z2n, z3n, z1n, z2f, z1f, z3f], [near, middle, *far])

    up, back, w_in, w_out = work(weights, [own, fx, fz, fzx], (low, up_map), width, rank, True)
    cross_up, cross_back = work((w_in, w_out), [fy, fxy, fzy, fzxy], (fy,), width, rank, False)

    back = (back + over_y(cross_back).astype(F32)).astype(BF)
    backs = [back, over_x(back), over_low(back), over_xlow(back)]
    cross_up = plus(over_y(cross_up), over_yhalf(cross_up))
    up = jnp.concatenate([plus(up, over_half(up)), cross_up], axis=1)
    down = down_half(backs, [own, fx, fz, fzx], width)
    down = plus(down, over_half(down))
    ups = [up, over_x(up), over_low(up), over_xlow(up)]
    downs = [down, over_x(down)]
    up_gradient, down_gradient = spread(ups, downs, block)
    return (down_gradient.transpose(0, 2, 1), up_gradient)


def gathered(frames, gain, first, second, down_map, up_map, lengths, cotangent):
    members = lax.axis_size("member")
    normed = normalize(frames[0], gain)
    low = dot(normed, down_map[0]).astype(BF)
    positions = jnp.arange(BUCKET, dtype=jnp.int32)
    mask = (positions[None, :] < lengths[0][:, None]).reshape(-1)
    masked = cotangent[0] * mask.astype(BF)[:, None]
    rows = normed.shape[0]
    up_slices = lax.all_to_all(up_map, "member", split_axis=2, concat_axis=0, tiled=True)
    all_normed = lax.all_gather(normed, "member", axis=0, tiled=True)
    all_low = lax.all_gather(low, "member", axis=0, tiled=True).reshape(members, rows, -1)
    all_masked = lax.all_gather(masked, "member", axis=0, tiled=True)
    term = jnp.einsum("dgs,dsb->dgb", all_low, up_slices, preferred_element_type=F32)
    pre = term.reshape(members * rows, -1) + dot(
        all_normed, lax.all_gather(first, "fsdp", axis=0, tiled=True)
    )
    dhid = 0.5 * dot(all_masked, lax.all_gather(second, "fsdp", axis=1, tiled=True), ((1,), (1,)))
    dpre = swish_gradient(pre, dhid).reshape(members, rows, -1)
    up_partial = jnp.einsum("jnz,jnv->jzv", all_low, dpre, preferred_element_type=F32)
    back_partial = jnp.einsum("yha,ywa->yhw", dpre, up_slices, preferred_element_type=F32)
    back = lax.psum_scatter(back_partial, "member", scatter_dimension=0, tiled=True)[0].astype(BF)
    up = lax.all_to_all(lax.psum(up_partial, "fsdp"), "member", split_axis=0, concat_axis=2, tiled=True)
    down = lax.psum(dot(normed, back, ((0,), (0,))), "fsdp")
    return (down[None], up)


def solution(mesh):
    in_specs = (
        P("member", "fsdp", None),
        P(),
        P("fsdp", "member"),
        P("member", "fsdp"),
        P("member", None, None),
        P("member", None, None),
        P("member", "fsdp"),
        P("member", "fsdp", None),
    )
    out_specs = (P("member", None, None), P("member", None, None))
    paired = mesh.shape["fsdp"] == 8 and mesh.shape["member"] == 4
    return jax.shard_map(
        paired_halves if paired else gathered,
        mesh=mesh,
        in_specs=in_specs,
        out_specs=out_specs,
        check_vma=False,
    )
```
